512 devices in a mesh: group: 8 (over y, core), ctx: 64 (over x, z).
Axes of the slice: x: 4, y: 4, z: 16, core: 2. Of those that a mesh axis runs over, the one named last changes fastest.
Arguments:
- query: bfloat16 [8, 4096, 4096], P('group', 'ctx'), may hold values from -6 to 6
- keys: bfloat16 [8, 4096, 4096], P('group', 'ctx'), may hold values from -6 to 6
- values: bfloat16 [8, 4096, 4096], P('group', 'ctx'), may hold values from -6 to 6
- decay_exp: int32 [32], replicated, may hold values from 0 to 10
- gain: float32 [4096], replicated, may hold values from 0.1 to 1.9
- route: int32 [8, 64, 8], P(None, 'ctx'), may hold values from 0 to 63, as said below
Outputs:
- mixed: bfloat16 [8, 4096, 4096], P('group', 'ctx')
The draws below stay inside these ranges and needn't reach their ends.
Inputs may be any that keep to these rules, and one draw needn't show every extreme that they name: For every context index c, route[:, c, :] names each place 0 to 63 exactly once.
All inputs are finite; a program needn't handle non-finite values.
Results may differ from the reference program's by a relative error of at most 0.0056.
Values may be sent and summed in bfloat16 or wider, within the bound.
No kernel may reach another device: no remote copies, remote signals or barrier semaphores. Data moves between devices by JAX's collectives and lax.ppermute only.
A program may use at most 64 MiB of HBM per device.

```python
import jax
import jax.numpy as jnp
from jax import lax

H = 32
E = 128
BLOCK = 512
SEQ = 32768
STORE = 4096
HD = 4096
ROW = 8
N_GROUP = 8
N_CTX = 64


def draw_route(key, part):
    key = jax.random.fold_in(key, 7)
    subkeys = jax.random.split(key, N_CTX)
    perms = jax.vmap(lambda subkey: jax.random.permutation(subkey, N_GROUP * N_GROUP))(subkeys)
    shaped = perms.astype(jnp.int32).reshape(N_CTX, N_GROUP, N_GROUP)
    return jnp.transpose(shaped, (1, 0, 2))


def place_ends(values, stream_key, low, largest):
    extent = values.shape
    spot = [jax.random.randint(jax.random.fold_in(stream_key, axis), (), 0, extent[axis]) for axis in range(len(extent))]
    values = values.at[tuple(spot)].set(low)
    longest = extent.index(max(extent))
    spot[longest] = (spot[longest] + 1) % extent[longest]
    return values.at[tuple(spot)].set(largest)


def block_levels(rng, extent, cuts, least, largest):
    loudness = 1.0
    for axis_at, blocks in cuts:
        draws = jax.random.uniform(jax.random.fold_in(jax.random.fold_in(rng, 6), axis_at), (blocks,), jnp.float32, least / len(cuts), largest / len(cuts))
        loudness = loudness * jnp.repeat(jnp.exp(draws), extent[axis_at] // blocks).reshape((-1,) + (1,) * (len(extent) - 1 - axis_at))
    return loudness


def scatter_about(rng, dims, deviation, bound, cuts=(), kind=jnp.bfloat16):
    factor_of = block_levels(rng, dims, cuts, -0.22, 0.18) if cuts else 1.0
    array = jax.random.normal(rng, dims, jnp.float32) * deviation * factor_of
    return jnp.minimum(jnp.maximum(array, -bound), bound).astype(kind)


def setup_inputs(seed: int = 0) -> dict:
    key_list = jax.random.split(jax.random.key(seed), 7)
    query = scatter_about(key_list[0], (N_GROUP, STORE, HD), 1.0, 6.0, ((0, 8), (1, 64)))
    keys = scatter_about(key_list[1], (N_GROUP, STORE, HD), 1.0, 6.0, ((0, 8), (1, 64)))
    values = scatter_about(key_list[2], (N_GROUP, STORE, HD), 1.0, 6.0, ((0, 8), (1, 64)))
    decay_exp = place_ends(jax.random.randint(key_list[3], (H,), 0, 11), jax.random.fold_in(key_list[3], 1), 0, 10).astype(jnp.int32)
    gain = jnp.clip(1.0 + 0.18 * jax.random.normal(key_list[4], (HD,), jnp.float32), 0.1, 1.9)
    route = draw_route(jax.random.fold_in(key_list[6], 71), 0)
    return dict(query=query, keys=keys, values=values, decay_exp=decay_exp, gain=gain, route=route)


def decay_tables(decay_exp):
    exponent = decay_exp.astype(jnp.float32)
    decay_rates = jnp.exp2(exponent * exponent / 8.0) / (4.0 * SEQ)
    position = jnp.arange(BLOCK, dtype=jnp.float32)
    offset = position[:, None] - position[None, :]
    causal = offset >= 0
    decay_mask = jnp.where(causal[None], jnp.exp(-decay_rates[:, None, None] * jnp.maximum(offset, 0.0)[None]), 0.0)
    end_weight = jnp.exp(-decay_rates[None, :] * (BLOCK - 1 - position)[:, None])
    start_weight = jnp.exp(-decay_rates[None, :] * (position + 1.0)[:, None])
    block_decay = jnp.exp(-decay_rates * BLOCK)
    return (decay_mask, end_weight, start_weight, block_decay)

def rounded(source):
    return lax.optimization_barrier(source.astype(jnp.bfloat16)).astype(jnp.float32)

def process_request(stacked, tables, gain_heads):
    decay_mask, end_weight, start_weight, block_decay = tables

    def block_step(carry_state, block_data):
        query_rows = block_data[0].reshape(BLOCK, H, E).astype(jnp.float32)
        key_rows = block_data[1].reshape(BLOCK, H, E).astype(jnp.float32)
        value_rows = block_data[2].reshape(BLOCK, H, E).astype(jnp.float32)
        scores = jnp.einsum('the,she->hts', query_rows, key_rows)
        weights = rounded(scores * decay_mask)
        within_block = jnp.einsum('hts,she->the', weights, value_rows)
        from_prior = jnp.einsum('the,hef->thf', query_rows, rounded(carry_state)) * start_weight[:, :, None]
        weighted = rounded(key_rows * end_weight[:, :, None])
        block_state = jnp.einsum('she,shf->hef', weighted, value_rows)
        new_state = block_decay[:, None, None] * carry_state + block_state
        combined = within_block + from_prior
        inverse_rms = lax.rsqrt(lax.optimization_barrier(jnp.mean(combined * combined, axis=-1, keepdims=True)) + 1e-06)
        normalized = combined * inverse_rms * gain_heads
        return (new_state, normalized.astype(jnp.bfloat16).reshape(BLOCK, HD))
    _, outputs = lax.scan(block_step, jnp.zeros((H, E, E), jnp.float32), stacked)
    return outputs

def reference(query, keys, values, decay_exp, gain, route):
    piece_order = jnp.transpose(route, (1, 0, 2)).reshape(N_CTX, N_GROUP * N_GROUP).astype(jnp.int32)
    inverse = jnp.argsort(piece_order, axis=-1).astype(jnp.int32)

    def to_request(source):
        pieces = source.reshape(N_GROUP, N_CTX, N_GROUP, ROW, HD)
        pieces = jnp.transpose(pieces, (1, 0, 2, 3, 4)).reshape(N_CTX, N_GROUP * N_GROUP, ROW, HD)
        picked = jnp.take_along_axis(pieces, inverse[:, :, None, None], axis=1)
        return picked.reshape(N_CTX, BLOCK, HD)
    tables = decay_tables(decay_exp)
    gain_heads = gain.reshape(H, E)
    stacked = (to_request(query), to_request(keys), to_request(values))
    outputs = process_request(stacked, tables, gain_heads)
    pieces = outputs.reshape(N_CTX, N_GROUP * N_GROUP, ROW, HD)
    stored = jnp.take_along_axis(pieces, piece_order[:, :, None, None], axis=1)
    stored = stored.reshape(N_CTX, N_GROUP, N_GROUP, ROW, HD)
    stored = jnp.transpose(stored, (1, 0, 2, 3, 4))
    return stored.reshape(N_GROUP, STORE, HD)
```

```python
import functools

import jax
import jax.numpy as jnp
import numpy as np
from jax import lax
from jax.experimental import pallas as pl
from jax.experimental.pallas import tpu as pltpu
from jax.sharding import Mesh
from jax.sharding import PartitionSpec as P

BF = jnp.bfloat16
F32 = jnp.float32
Z = 16
E = 128
ROW = 8


def vmem():
    return pl.BlockSpec(memory_space=pltpu.VMEM)


def smem():
    return pl.BlockSpec(memory_space=pltpu.SMEM)


def params(**more):
    return pltpu.CompilerParams(vmem_limit_bytes=48 * 1024 * 1024, **more)


def decay_of(exp_ref, head):
    exponent = jnp.full((1, E), exp_ref[head], jnp.int32).astype(F32)
    return jnp.exp2(exponent * exponent / 8.0)


def pack(tokens, pieces, where_ref, route_ref, query, keys, values, out):
    heads = out.shape[0]
    first = where_ref[0] * pieces
    token = lax.broadcasted_iota(jnp.int32, (ROW, E), 1) % tokens
    places = jnp.zeros((ROW, E), jnp.int32)
    for piece in range(pieces):
        places = jnp.where(token // ROW == piece, route_ref[first + piece], places)
    places = places.astype(F32).astype(BF)
    for head in range(heads):
        columns = slice(head * E, (head + 1) * E)
        for at, source in enumerate((query, keys, values)):
            out[head, at * tokens : (at + 1) * tokens, :] = source[0, :, columns]
        out[head, 3 * tokens :, :] = places


def row_positions(received, tokens, block):
    lane = lax.broadcasted_iota(jnp.int32, (ROW, E), 1)
    step = (lane % ROW).astype(F32)
    chunks = []
    for pair in range(received.shape[0] // 2):
        even = received[2 * pair, block, 3 * tokens :, :].astype(F32)
        odd = received[2 * pair + 1, block, 3 * tokens :, :].astype(F32)
        chunks.append(jnp.where(lane < tokens, even, odd) * float(ROW) + step)
    return chunks


def column_positions(chunks):
    return jnp.concatenate(
        [jnp.transpose(jnp.broadcast_to(chunk[:1, :], (E, E))) for chunk in chunks], axis=0
    )


def states(tokens, scale, where_ref, exp_ref, received, out):
    groups, blocks = received.shape[:2]
    length = groups * tokens
    decay = decay_of(exp_ref, where_ref[1]) * scale
    found = []
    for block in range(blocks):
        position = column_positions(row_positions(received, tokens, block))
        weight = jnp.exp(-decay * (length - 1.0 - position))
        key_rows = received[:, block, tokens : 2 * tokens, :].reshape(length, E)
        value_rows = received[:, block, 2 * tokens : 3 * tokens, :].reshape(length, E)
        weighted = (key_rows.astype(F32) * weight).astype(BF)
        found.append(
            lax.dot_general(
                weighted, value_rows, (((0,), (0,)), ((), ())), preferred_element_type=F32
            )
        )
    for at in range(out.shape[0]):
        rows = slice(at * ROW, (at + 1) * ROW)
        out[at] = jnp.concatenate([state[rows] for state in found], axis=0).astype(BF)


def scan(length, scale, where_ref, exp_ref, pieces, out):
    steps, rows = pieces.shape[:2]
    decay = jnp.exp(-decay_of(exp_ref, where_ref[1]) * scale * length)
    total = jnp.zeros((ROW, E), F32)
    priors = [[None] * (rows // ROW) for _ in range(steps)]
    loaded = [pieces[step].astype(F32) for step in range(steps)]
    for block in range(rows // ROW):
        for step in range(steps):
            priors[step][block] = total
            total = total * decay + loaded[step][block * ROW : (block + 1) * ROW]
    for step in range(steps):
        out[step] = jnp.concatenate(priors[step], axis=0).astype(BF)


def attend(tokens, scale, where_ref, exp_ref, gain, received, prior, out):
    groups, blocks = received.shape[:2]
    length = groups * tokens
    middle = length / 2.0
    head = where_ref[1]
    decay = decay_of(exp_ref, head) * scale
    scaling = gain[pl.ds(head, 1), :]
    prior_weight = jnp.exp(-decay * (middle + 1.0))
    for block in range(blocks):
        chunks = row_positions(received, tokens, block)
        row = jnp.concatenate([chunk[:1] for chunk in chunks], axis=1)
        key_weight = jnp.exp(jnp.concatenate([decay] * len(chunks), axis=1) * (row - middle))
        column = column_positions(chunks)
        query_weight = jnp.exp(-decay * (column - middle))
        query_rows = received[:, block, :tokens, :].reshape(length, E)
        key_rows = received[:, block, tokens : 2 * tokens, :].reshape(length, E)
        value_rows = received[:, block, 2 * tokens : 3 * tokens, :].reshape(length, E)
        rows = slice(block * ROW, (block + 1) * ROW)
        state = jnp.concatenate(
            [prior[at].astype(F32)[rows] for at in range(prior.shape[0])], axis=0
        ).astype(BF)
        scores = lax.dot_general(
            query_rows, key_rows, (((1,), (1,)), ((), ())), preferred_element_type=F32
        )
        weights = jnp.where(column[:, :1] >= row, scores * key_weight, 0.0).astype(BF)
        combined = jnp.dot(weights, value_rows, preferred_element_type=F32)
        combined += jnp.dot(query_rows, state, preferred_element_type=F32) * prior_weight
        combined *= query_weight
        square = jnp.mean(combined * combined, axis=-1, keepdims=True)
        normal = (combined * lax.rsqrt(square + 1e-06) * scaling).astype(BF)
        out[:, block] = normal.reshape(groups, tokens, E)


def unpack(received, out):
    for head in range(received.shape[0]):
        out[0, :, head * E : (head + 1) * E] = received[head]


def on_device(query, keys, values, decay_exp, gain, route):
    groups = lax.axis_size("group")
    rows = lax.axis_size("x")
    tokens, width = query.shape[1:]
    heads = decay_exp.shape[0]
    pieces = tokens // ROW
    length = tokens * groups
    scale = 1.0 / (4.0 * length * rows * Z)
    group = lax.axis_index("group")
    where = jnp.stack([group, group * rows + lax.axis_index("x")]).astype(jnp.int32)
    sent_rows = 3 * tokens + ROW
    steps = 4
    sent = pl.pallas_call(
        functools.partial(pack, tokens, pieces),
        grid=(steps,),
        in_specs=[smem(), smem()]
        + [pl.BlockSpec((1, tokens, width // steps), lambda i: (0, 0, i))] * 3,
        out_specs=pl.BlockSpec((heads // steps, sent_rows, E), lambda i: (i, 0, 0)),
        out_shape=jax.ShapeDtypeStruct((heads, sent_rows, E), BF),
        compiler_params=params(),
        name="pack",
    )(where, route.reshape(groups * pieces), query, keys, values)
    received = lax.all_to_all(sent, ("group", "x"), split_axis=0, concat_axis=0, tiled=True)
    received = received.reshape(groups, rows, sent_rows, E)
    sliced = pl.pallas_call(
        functools.partial(states, tokens, scale),
        in_specs=[smem(), smem(), vmem()],
        out_specs=vmem(),
        out_shape=jax.ShapeDtypeStruct((Z, rows * ROW, E), BF),
        compiler_params=params(),
        name="states",
    )(where, decay_exp, received)
    sliced = lax.all_to_all(sliced, "z", split_axis=0, concat_axis=0, tiled=True)
    priors = pl.pallas_call(
        functools.partial(scan, length, scale),
        in_specs=[smem(), smem(), vmem()],
        out_specs=vmem(),
        out_shape=jax.ShapeDtypeStruct((Z, rows * ROW, E), BF),
        compiler_params=params(),
        name="scan",
    )(where, decay_exp, sliced)
    priors = lax.all_to_all(priors, "z", split_axis=0, concat_axis=0, tiled=True)
    mixed = pl.pallas_call(
        functools.partial(attend, tokens, scale),
        in_specs=[smem(), smem(), vmem(), vmem(), vmem()],
        out_specs=vmem(),
        out_shape=jax.ShapeDtypeStruct((groups, rows, tokens, E), BF),
        compiler_params=params(),
        name="attend",
    )(where, decay_exp, gain.reshape(heads, E), received, priors)
    mixed = mixed.reshape(heads, tokens, E)
    mixed = lax.all_to_all(mixed, ("group", "x"), split_axis=0, concat_axis=0, tiled=True)
    return pl.pallas_call(
        unpack,
        grid=(steps,),
        in_specs=[pl.BlockSpec((heads // steps, tokens, E), lambda i: (i, 0, 0))],
        out_specs=pl.BlockSpec((1, tokens, width // steps), lambda i: (0, 0, i)),
        out_shape=jax.ShapeDtypeStruct((1, tokens, width), BF),
        compiler_params=params(),
        name="unpack",
    )(mixed)


def solution(mesh):
    devices = np.asarray(mesh.devices)
    split = Mesh(devices.reshape(devices.shape[0], -1, Z), ("group", "x", "z"))
    ctx = ("x", "z")
    stored = P("group", ctx, None)
    in_specs = (stored, stored, stored, P(), P(), P(None, ctx, None))
    return jax.shard_map(
        on_device, mesh=split, in_specs=in_specs, out_specs=stored, check_vma=False
    )
```

```python
import functools

import jax
import jax.numpy as jnp
import numpy as np
from jax import lax
from jax.experimental import pallas as pl
from jax.experimental.pallas import tpu as pltpu
from jax.sharding import Mesh
from jax.sharding import PartitionSpec as P

BF = jnp.bfloat16
F32 = jnp.float32
Z = 16
E = 128
ROW = 8


def vmem():
    return pl.BlockSpec(memory_space=pltpu.VMEM)


def smem():
    return pl.BlockSpec(memory_space=pltpu.SMEM)


def params(mebibytes=48):
    return pltpu.CompilerParams(vmem_limit_bytes=mebibytes * 1024 * 1024)


def my_head():
    return lax.axis_index("group") * lax.axis_size("x") + lax.axis_index("x")


def anywhere():
    return pl.BlockSpec(memory_space=pl.ANY)


def pack(tokens, pieces, route, query, keys, values, out, staged, route_ref, in_sems, out_sems, sem):
    heads = out.shape[0]
    parts = in_sems.shape[0]
    fetch = pltpu.make_async_copy(route, route_ref, sem)
    fetch.start()
    span = heads // parts
    for part in range(parts):
        for head in range(part * span, (part + 1) * span):
            for at, source in enumerate((query, keys, values)):
                pltpu.make_async_copy(
                    source.at[0, :, pl.ds(head * E, E)],
                    staged.at[head, pl.ds(at * tokens, tokens), :],
                    in_sems.at[part],
                ).start()
    token = lax.broadcasted_iota(jnp.int32, (ROW, E), 1) % tokens
    places = jnp.zeros((ROW, E), jnp.int32)
    group = lax.axis_index("group")
    fetch.wait()
    for piece in range(pieces):
        places = jnp.where(token // ROW == piece, route_ref[group, 0, piece], places)
    places = places.astype(F32).astype(BF)
    for head in range(heads):
        staged[head, 3 * tokens :, :] = places
    copies = []
    for part in range(parts):
        some = pl.ds(part * span, span)
        landed = staged.at[some, pl.ds(0, 3 * tokens), :]
        pltpu.make_async_copy(landed, landed, in_sems.at[part]).wait()
        copies.append(pltpu.make_async_copy(staged.at[some], out.at[some], out_sems.at[part]))
        copies[-1].start()
    for copy in copies:
        copy.wait()


def row_positions(received, tokens, block):
    lane = lax.broadcasted_iota(jnp.int32, (ROW, E), 1)
    step = (lane % ROW).astype(F32)
    chunks = []
    for pair in range(received.shape[0] // 2):
        even = received[2 * pair, block, 3 * tokens :, :].astype(F32)
        odd = received[2 * pair + 1, block, 3 * tokens :, :].astype(F32)
        chunks.append(jnp.where(lane < tokens, even, odd) * float(ROW) + step)
    return chunks


def column_positions(chunks):
    return jnp.concatenate(
        [jnp.transpose(jnp.broadcast_to(chunk[:1, :], (E, E))) for chunk in chunks], axis=0
    )


def states(tokens, scale, exp_ref, gain, received, out, constants):
    groups, blocks = received.shape[:2]
    length = groups * tokens
    head = my_head()
    exponent = jnp.full((ROW, E), exp_ref[head], jnp.int32).astype(F32)
    decay = jnp.exp2(exponent * exponent / 8.0) * scale
    constants[0] = decay
    constants[1] = jnp.broadcast_to(gain[pl.ds(head, 1), :], (ROW, E))
    wide = jnp.concatenate([decay[:1]] * (length // E), axis=1)
    found = []
    for block in range(blocks):
        chunks = row_positions(received, tokens, block)
        position = jnp.concatenate([chunk[:1] for chunk in chunks], axis=1)
        weight = jnp.exp(-wide * (length - 1.0 - position))
        key_rows = received[:, block, tokens : 2 * tokens, :].reshape(length, E)
        value_rows = received[:, block, 2 * tokens : 3 * tokens, :].reshape(length, E)
        weighted = (jnp.transpose(key_rows).astype(F32) * weight).astype(BF)
        found.append(jnp.dot(weighted, value_rows, preferred_element_type=F32))
    for at in range(out.shape[0]):
        rows = slice(at * ROW, (at + 1) * ROW)
        out[at] = jnp.concatenate([state[rows] for state in found], axis=0).astype(BF)


def scan(length, constants, pieces, out):
    steps, rows = pieces.shape[:2]
    decay = jnp.exp(-constants[0] * length)
    total = jnp.zeros((ROW, E), F32)
    priors = [[None] * (rows // ROW) for _ in range(steps)]
    loaded = [pieces[step].astype(F32) for step in range(steps)]
    for block in range(rows // ROW):
        for step in range(steps):
            priors[step][block] = total
            total = total * decay + loaded[step][block * ROW : (block + 1) * ROW]
    for step in range(steps):
        out[step] = jnp.concatenate(priors[step], axis=0).astype(BF)


def within(tokens, constants, received, out, query_weight):
    groups, blocks = received.shape[:2]
    length = groups * tokens
    middle = length / 2.0
    decay = constants[0][:1]
    prior_weight = jnp.exp(-decay * (middle + 1.0))
    lane = lax.broadcasted_iota(jnp.int32, (length, E), 1)
    query_weights = jnp.zeros((length, E), F32)
    for block in range(blocks):
        chunks = row_positions(received, tokens, block)
        row = jnp.concatenate([chunk[:1] for chunk in chunks], axis=1)
        key_weight = jnp.exp(jnp.concatenate([decay] * len(chunks), axis=1) * (row - middle))
        column = column_positions(chunks)
        weight = jnp.exp(-decay * (column - middle))
        query_rows = received[:, block, :tokens, :].reshape(length, E)
        key_rows = received[:, block, tokens : 2 * tokens, :].reshape(length, E)
        value_rows = received[:, block, 2 * tokens : 3 * tokens, :].reshape(length, E)
        scores = lax.dot_general(
            query_rows, key_rows, (((1,), (1,)), ((), ())), preferred_element_type=F32
        )
        weights = jnp.where(column[:, :1] >= row, scores * key_weight, 0.0).astype(BF)
        out[block] = jnp.dot(weights, value_rows, preferred_element_type=F32) * weight
        query_weights = jnp.where(lane == block, weight * prior_weight, query_weights)
    query_weight[...] = query_weights


def finish(tokens, constants, received, prior, sums, query_weight, out):
    groups, blocks = received.shape[:2]
    scaling = constants[1][:1]
    for block in range(blocks):
        query_rows = received[:, block, :tokens, :].reshape(groups * tokens, E)
        rows = slice(block * ROW, (block + 1) * ROW)
        state = jnp.concatenate(
            [prior[at].astype(F32)[rows] for at in range(prior.shape[0])], axis=0
        ).astype(BF)
        combined = jnp.dot(query_rows, state, preferred_element_type=F32)
        combined = sums[block] + combined * query_weight[:, block : block + 1]
        square = jnp.mean(combined * combined, axis=-1, keepdims=True)
        normal = (combined * lax.rsqrt(square + 1e-06) * scaling).astype(BF)
        out[:, block] = normal.reshape(groups, tokens, E)


def unpack(received, out, sem):
    heads, tokens = received.shape[:2]
    for head in range(heads):
        columns = out.at[0, :, pl.ds(head * E, E)]
        pltpu.make_async_copy(received.at[head], columns, sem).start()
    pltpu.make_async_copy(received, received, sem).wait()


def on_device(query, keys, values, decay_exp, gain, route):
    groups = lax.axis_size("group")
    rows = lax.axis_size("x")
    tokens, width = query.shape[1:]
    heads = decay_exp.shape[0]
    pieces = tokens // ROW
    length = tokens * groups
    scale = 1.0 / (4.0 * length * rows * Z)
    sent_rows = 3 * tokens + ROW
    parts = 4
    sent = pl.pallas_call(
        functools.partial(pack, tokens, pieces),
        in_specs=[anywhere()] * 4,
        out_specs=anywhere(),
        out_shape=jax.ShapeDtypeStruct((heads, sent_rows, E), BF),
        scratch_shapes=[
            pltpu.VMEM((heads, sent_rows, E), BF),
            pltpu.SMEM(route.shape, jnp.int32),
            pltpu.SemaphoreType.DMA((parts,)),
            pltpu.SemaphoreType.DMA((parts,)),
            pltpu.SemaphoreType.DMA,
        ],
        compiler_params=params(62),
        name="pack",
    )(route, query, keys, values)
    received = lax.all_to_all(sent, ("group", "x"), split_axis=0, concat_axis=0, tiled=True)
    received = received.reshape(groups, rows, sent_rows, E)
    sliced, constants = pl.pallas_call(
        functools.partial(states, tokens, scale),
        in_specs=[smem(), vmem(), vmem()],
        out_specs=(vmem(), vmem()),
        out_shape=(
            jax.ShapeDtypeStruct((Z, rows * ROW, E), BF),
            jax.ShapeDtypeStruct((2, ROW, E), F32),
        ),
        compiler_params=params(),
        name="states",
    )(decay_exp, gain.reshape(heads, E), received)
    sliced = lax.all_to_all(sliced, "z", split_axis=0, concat_axis=0, tiled=True)
    priors = pl.pallas_call(
        functools.partial(scan, length),
        in_specs=[vmem(), vmem()],
        out_specs=vmem(),
        out_shape=jax.ShapeDtypeStruct((Z, rows * ROW, E), BF),
        compiler_params=params(),
        name="scan",
    )(constants, sliced)
    priors = lax.all_to_all(priors, "z", split_axis=0, concat_axis=0, tiled=True)
    sums, query_weight = pl.pallas_call(
        functools.partial(within, tokens),
        in_specs=[vmem(), vmem()],
        out_specs=(vmem(), vmem()),
        out_shape=(
            jax.ShapeDtypeStruct((rows, length, E), F32),
            jax.ShapeDtypeStruct((length, E), F32),
        ),
        compiler_params=params(),
        cost_estimate=pl.CostEstimate(
            flops=4 * rows * length * length * E,
            bytes_accessed=4 * rows * length * E * 4,
            transcendentals=rows * length * E,
        ),
        name="within",
    )(constants, received)
    mixed = pl.pallas_call(
        functools.partial(finish, tokens),
        in_specs=[vmem()] * 5,
        out_specs=vmem(),
        out_shape=jax.ShapeDtypeStruct((groups, rows, tokens, E), BF),
        compiler_params=params(),
        name="finish",
    )(constants, received, priors, sums, query_weight)
    mixed = mixed.reshape(heads, tokens, E)
    mixed = lax.all_to_all(mixed, ("group", "x"), split_axis=0, concat_axis=0, tiled=True)
    return pl.pallas_call(
        unpack,
        in_specs=[anywhere()],
        out_specs=anywhere(),
        out_shape=jax.ShapeDtypeStruct((1, tokens, width), BF),
        scratch_shapes=[pltpu.SemaphoreType.DMA],
        compiler_params=params(),
        name="unpack",
    )(mixed)


def solution(mesh):
    devices = np.asarray(mesh.devices)
    split = Mesh(devices.reshape(devices.shape[0], -1, Z), ("group", "x", "z"))
    ctx = ("x", "z")
    stored = P("group", ctx, None)
    in_specs = (stored, stored, stored, P(), P(), P(None, ctx, None))
    return jax.shard_map(
        on_device, mesh=split, in_specs=in_specs, out_specs=stored, check_vma=False
    )
```

```python
import functools

import jax
import jax.numpy as jnp
import numpy as np
from jax import lax
from jax.experimental import pallas as pl
from jax.experimental.pallas import tpu as pltpu
from jax.sharding import Mesh
from jax.sharding import PartitionSpec as P

BF = jnp.bfloat16
F32 = jnp.float32
Z = 16
E = 128
ROW = 8


def vmem():
    return pl.BlockSpec(memory_space=pltpu.VMEM)


def params(mebibytes=48):
    return pltpu.CompilerParams(vmem_limit_bytes=mebibytes * 1024 * 1024)


def anywhere():
    return pl.BlockSpec(memory_space=pl.ANY)


def pack(tokens, pieces, route, query, keys, values, out, staged, route_ref, in_sems, out_sems, sem):
    heads = out.shape[0]
    parts = in_sems.shape[0]
    fetch = pltpu.make_async_copy(route, route_ref, sem)
    fetch.start()
    span = heads // parts
    for part in range(parts):
        for head in range(part * span, (part + 1) * span):
            for at, source in enumerate((query, keys, values)):
                pltpu.make_async_copy(
                    source.at[0, :, pl.ds(head * E, E)],
                    staged.at[head, pl.ds(at * tokens, tokens), :],
                    in_sems.at[part],
                ).start()
    token = lax.broadcasted_iota(jnp.int32, (ROW, E), 1) % tokens
    places = jnp.zeros((ROW, E), jnp.int32)
    group = lax.axis_index("group")
    fetch.wait()
    for piece in range(pieces):
        places = jnp.where(token // ROW == piece, route_ref[group, 0, piece], places)
    places = places.astype(F32).astype(BF)
    for head in range(heads):
        staged[head, 3 * tokens :, :] = places
    copies = []
    for part in range(parts):
        some = pl.ds(part * span, span)
        landed = staged.at[some, pl.ds(0, 3 * tokens), :]
        pltpu.make_async_copy(landed, landed, in_sems.at[part]).wait()
        copies.append(pltpu.make_async_copy(staged.at[some], out.at[some], out_sems.at[part]))
        copies[-1].start()
    for copy in copies:
        copy.wait()


def row_positions(received, tokens, block):
    lane = lax.broadcasted_iota(jnp.int32, (ROW, E), 1)
    step = (lane % ROW).astype(F32)
    chunks = []
    for pair in range(received.shape[0] // 2):
        even = received[2 * pair, block, 3 * tokens :, :].astype(F32)
        odd = received[2 * pair + 1, block, 3 * tokens :, :].astype(F32)
        chunks.append(jnp.where(lane < tokens, even, odd) * float(ROW) + step)
    return chunks


def column_positions(chunks):
    return jnp.concatenate(
        [jnp.transpose(jnp.broadcast_to(chunk[:1, :], (E, E))) for chunk in chunks], axis=0
    )


def states(tokens, scale, exponents, gain, received, out, constants):
    groups, blocks = received.shape[:2]
    length = groups * tokens
    heads = exponents.shape[1]
    head = lax.axis_index("group") * lax.axis_size("x") + lax.axis_index("x")
    mine = lax.broadcasted_iota(jnp.int32, (1, heads), 1) == head
    exponent = jnp.sum(jnp.where(mine, exponents[...], 0).astype(F32), axis=1, keepdims=True)
    exponent = jnp.broadcast_to(exponent, (ROW, E))
    decay = jnp.exp2(exponent * exponent / 8.0) * scale
    constants[0] = decay
    constants[1] = jnp.broadcast_to(gain[pl.ds(head, 1), :], (ROW, E))
    wide = jnp.concatenate([decay[:1]] * (length // E), axis=1)
    found = []
    for block in range(blocks):
        chunks = row_positions(received, tokens, block)
        position = jnp.concatenate([chunk[:1] for chunk in chunks], axis=1)
        weight = jnp.exp(-wide * (length - 1.0 - position))
        key_rows = received[:, block, tokens : 2 * tokens, :].reshape(length, E)
        value_rows = received[:, block, 2 * tokens : 3 * tokens, :].reshape(length, E)
        weighted = (jnp.transpose(key_rows).astype(F32) * weight).astype(BF)
        found.append(jnp.dot(weighted, value_rows, preferred_element_type=F32))
    for at in range(out.shape[0]):
        rows = slice(at * ROW, (at + 1) * ROW)
        out[at] = jnp.concatenate([state[rows] for state in found], axis=0).astype(BF)


def scan(length, constants, pieces, out):
    steps, rows = pieces.shape[:2]
    blocks = rows // ROW
    decay = jnp.exp(-constants[0] * length)
    decays = jnp.concatenate([decay] * blocks, axis=0)
    total = jnp.zeros((rows, E), F32)
    priors = []
    for step in range(steps):
        priors.append(total)
        total = total * decays + pieces[step].astype(F32)
    whole = jnp.exp(-constants[0] * (length * steps))
    carry = jnp.zeros((ROW, E), F32)
    carries = []
    for block in range(blocks):
        carries.append(carry)
        carry = carry * whole + total[block * ROW : (block + 1) * ROW]
    carry = jnp.concatenate(carries, axis=0)
    for step in range(steps):
        out[step] = (priors[step] + carry).astype(BF)
        carry = carry * decays


def within(tokens, constants, received, out, query_weight):
    groups, blocks = received.shape[:2]
    length = groups * tokens
    middle = length / 2.0
    decay = constants[0][:1]
    prior_weight = jnp.exp(-decay * (middle + 1.0))
    lane = lax.broadcasted_iota(jnp.int32, (length, E), 1)
    query_weights = jnp.zeros((length, E), F32)
    for block in range(blocks):
        chunks = row_positions(received, tokens, block)
        row = jnp.concatenate([chunk[:1] for chunk in chunks], axis=1)
        key_weight = jnp.exp(jnp.concatenate([decay] * len(chunks), axis=1) * (row - middle))
        column = column_positions(chunks)
        weight = jnp.exp(-decay * (column - middle))
        query_rows = received[:, block, :tokens, :].reshape(length, E)
        key_rows = received[:, block, tokens : 2 * tokens, :].reshape(length, E)
        value_rows = received[:, block, 2 * tokens : 3 * tokens, :].reshape(length, E)
        scores = lax.dot_general(
            query_rows, key_rows, (((1,), (1,)), ((), ())), preferred_element_type=F32
        )
        weights = jnp.where(column[:, :1] >= row, scores * key_weight, 0.0).astype(BF)
        out[block] = jnp.dot(weights, value_rows, preferred_element_type=F32) * weight
        query_weights = jnp.where(lane == block, weight * prior_weight, query_weights)
    query_weight[...] = query_weights


def finish(tokens, constants, received, prior, sums, query_weight, out):
    groups, blocks = received.shape[:2]
    scaling = constants[1][:1]
    ones = jnp.full((E, E), 1.0 / E, BF)
    for block in range(blocks):
        query_rows = received[:, block, :tokens, :].reshape(groups * tokens, E)
        rows = slice(block * ROW, (block + 1) * ROW)
        state = jnp.concatenate(
            [prior[at].astype(F32)[rows] for at in range(prior.shape[0])], axis=0
        ).astype(BF)
        combined = jnp.dot(query_rows, state, preferred_element_type=F32)
        combined = sums[block] + combined * query_weight[:, block : block + 1]
        square = jnp.dot(
            (combined * combined).astype(BF), ones, preferred_element_type=F32
        )
        normal = (combined * lax.rsqrt(square + 1e-06) * scaling).astype(BF)
        out[:, block] = normal.reshape(groups, tokens, E)


def unpack(received, out, sem):
    heads, tokens = received.shape[:2]
    for head in range(heads):
        columns = out.at[0, :, pl.ds(head * E, E)]
        pltpu.make_async_copy(received.at[head], columns, sem).start()
    pltpu.make_async_copy(received, received, sem).wait()


def on_device(query, keys, values, decay_exp, gain, route):
    groups = lax.axis_size("group")
    rows = lax.axis_size("x")
    tokens, width = query.shape[1:]
    heads = decay_exp.shape[0]
    pieces = tokens // ROW
    length = tokens * groups
    scale = 1.0 / (4.0 * length * rows * Z)
    sent_rows = 3 * tokens + ROW
    parts = 4
    sent = pl.pallas_call(
        functools.partial(pack, tokens, pieces),
        in_specs=[anywhere()] * 4,
        out_specs=anywhere(),
        out_shape=jax.ShapeDtypeStruct((heads, sent_rows, E), BF),
        scratch_shapes=[
            pltpu.VMEM((heads, sent_rows, E), BF),
            pltpu.SMEM(route.shape, jnp.int32),
            pltpu.SemaphoreType.DMA((parts,)),
            pltpu.SemaphoreType.DMA((parts,)),
            pltpu.SemaphoreType.DMA,
        ],
        compiler_params=params(62),
        name="pack",
    )(route, query, keys, values)
    received = lax.all_to_all(sent, ("group", "x"), split_axis=0, concat_axis=0, tiled=True)
    received = received.reshape(groups, rows, sent_rows, E)
    sliced, constants = pl.pallas_call(
        functools.partial(states, tokens, scale),
        in_specs=[vmem(), vmem(), vmem()],
        out_specs=(vmem(), vmem()),
        out_shape=(
            jax.ShapeDtypeStruct((Z, rows * ROW, E), BF),
            jax.ShapeDtypeStruct((2, ROW, E), F32),
        ),
        compiler_params=params(),
        name="states",
    )(decay_exp.reshape(1, heads), gain.reshape(heads, E), received)
    sliced = lax.all_to_all(sliced, "z", split_axis=0, concat_axis=0, tiled=True)
    priors = pl.pallas_call(
        functools.partial(scan, length),
        in_specs=[vmem(), vmem()],
        out_specs=vmem(),
        out_shape=jax.ShapeDtypeStruct((Z, rows * ROW, E), BF),
        compiler_params=params(),
        name="scan",
    )(constants, sliced)
    priors = lax.all_to_all(priors, "z", split_axis=0, concat_axis=0, tiled=True)
    sums, query_weight = pl.pallas_call(
        functools.partial(within, tokens),
        in_specs=[vmem(), vmem()],
        out_specs=(vmem(), vmem()),
        out_shape=(
            jax.ShapeDtypeStruct((rows, length, E), F32),
            jax.ShapeDtypeStruct((length, E), F32),
        ),
        compiler_params=params(),
        cost_estimate=pl.CostEstimate(
            flops=4 * rows * length * length * E,
            bytes_accessed=4 * rows * length * E * 4,
            transcendentals=rows * length * E,
        ),
        name="within",
    )(constants, received)
    mixed = pl.pallas_call(
        functools.partial(finish, tokens),
        in_specs=[vmem()] * 5,
        out_specs=vmem(),
        out_shape=jax.ShapeDtypeStruct((groups, rows, tokens, E), BF),
        compiler_params=params(),
        name="finish",
    )(constants, received, priors, sums, query_weight)
    mixed = mixed.reshape(heads, tokens, E)
    mixed = lax.all_to_all(mixed, ("group", "x"), split_axis=0, concat_axis=0, tiled=True)
    return pl.pallas_call(
        unpack,
        in_specs=[anywhere()],
        out_specs=anywhere(),
        out_shape=jax.ShapeDtypeStruct((1, tokens, width), BF),
        scratch_shapes=[pltpu.SemaphoreType.DMA],
        compiler_params=params(),
        name="unpack",
    )(mixed)


def solution(mesh):
    devices = np.asarray(mesh.devices)
    split = Mesh(devices.reshape(devices.shape[0], -1, Z), ("group", "x", "z"))
    ctx = ("x", "z")
    stored = P("group", ctx, None)
    in_specs = (stored, stored, stored, P(), P(), P(None, ctx, None))
    return jax.shard_map(
        on_device, mesh=split, in_specs=in_specs, out_specs=stored, check_vma=False
    )
```

```python
import functools

import jax
import jax.numpy as jnp
import numpy as np
from jax import lax
from jax.experimental import pallas as pl
from jax.experimental.pallas import tpu as pltpu
from jax.sharding import Mesh
from jax.sharding import PartitionSpec as P

BF = jnp.bfloat16
F32 = jnp.float32
QUADS = 4
QUAD = 4
FIRST_GROUP, FIRST_X, FIRST_QUAD, FIRST_BEFORE, FIRST_AFTER = 6, 2, 2, 0, 3
E = 128
ROW = 8


def vmem():
    return pl.BlockSpec(memory_space=pltpu.VMEM)


def params(mebibytes=48):
    return pltpu.CompilerParams(vmem_limit_bytes=mebibytes * 1024 * 1024)


def anywhere():
    return pl.BlockSpec(memory_space=pl.ANY)


def pack(tokens, pieces, route, query, keys, values, out, staged, route_ref, in_sems, out_sems, sem):
    heads = out.shape[0]
    first = FIRST_GROUP * lax.axis_size("x") + FIRST_X
    parts = in_sems.shape[0]
    fetch = pltpu.make_async_copy(route, route_ref, sem)
    fetch.start()
    span = heads // parts
    for part in range(parts):
        for head in range(part * span, (part + 1) * span):
            for at, source in enumerate((query, keys, values)):
                pltpu.make_async_copy(
                    source.at[0, :, pl.ds((head ^ first) * E, E)],
                    staged.at[head, pl.ds(at * tokens, tokens), :],
                    in_sems.at[part],
                ).start()
    token = lax.broadcasted_iota(jnp.int32, (ROW, E), 1) % tokens
    places = jnp.zeros((ROW, E), jnp.int32)
    group = lax.axis_index("group")
    fetch.wait()
    for piece in range(pieces):
        places = jnp.where(token // ROW == piece, route_ref[group, 0, piece], places)
    places = places.astype(F32).astype(BF)
    for head in range(heads):
        staged[head, 3 * tokens :, :] = places
    copies = []
    for part in range(parts):
        some = pl.ds(part * span, span)
        landed = staged.at[some, pl.ds(0, 3 * tokens), :]
        pltpu.make_async_copy(landed, landed, in_sems.at[part]).wait()
        copies.append(pltpu.make_async_copy(staged.at[some], out.at[some], out_sems.at[part]))
        copies[-1].start()
    for copy in copies:
        copy.wait()


def row_positions(received, tokens, block):
    lane = lax.broadcasted_iota(jnp.int32, (ROW, E), 1)
    step = (lane % ROW).astype(F32)
    chunks = []
    for pair in range(received.shape[0] // 2):
        even = received[2 * pair, block, 3 * tokens :, :].astype(F32)
        odd = received[2 * pair + 1, block, 3 * tokens :, :].astype(F32)
        chunks.append(jnp.where(lane < tokens, even, odd) * float(ROW) + step)
    return chunks


def column_positions(chunks):
    return jnp.concatenate(
        [jnp.transpose(jnp.broadcast_to(chunk[:1, :], (E, E))) for chunk in chunks], axis=0
    )


def states(tokens, scale, exponents, gain, received, out, constants):
    groups, blocks = received.shape[:2]
    length = groups * tokens
    heads = exponents.shape[1]
    head = lax.axis_index("group") * lax.axis_size("x") + lax.axis_index("x")
    mine = lax.broadcasted_iota(jnp.int32, (1, heads), 1) == head
    exponent = jnp.sum(jnp.where(mine, exponents[...], 0).astype(F32), axis=1, keepdims=True)
    exponent = jnp.broadcast_to(exponent, (ROW, E))
    decay = jnp.exp2(exponent * exponent / 8.0) * scale
    constants[0] = decay
    constants[1] = jnp.broadcast_to(gain[pl.ds(head, 1), :], (ROW, E))
    wide = jnp.concatenate([decay[:1]] * (length // E), axis=1)
    found = []
    for block in range(blocks):
        chunks = row_positions(received, tokens, block)
        position = jnp.concatenate([chunk[:1] for chunk in chunks], axis=1)
        weight = jnp.exp(-wide * (length - 1.0 - position))
        key_rows = received[:, block, tokens : 2 * tokens, :].reshape(length, E)
        value_rows = received[:, block, 2 * tokens : 3 * tokens, :].reshape(length, E)
        weighted = (jnp.transpose(key_rows).astype(F32) * weight).astype(BF)
        found.append(jnp.dot(weighted, value_rows, preferred_element_type=F32))
    span = E // out.shape[0]
    for at in range(out.shape[0]):
        rows = slice(at * span, (at + 1) * span)
        out[at] = jnp.concatenate(
            [found[row ^ FIRST_X][rows] for row in range(blocks)], axis=0
        ).astype(BF)


def totals(length, constants, pieces, out):
    decay = jnp.exp(-constants[0][:1] * length)
    total = pieces[FIRST_BEFORE].astype(F32)
    for step in range(1, pieces.shape[0]):
        total = total * decay + pieces[step ^ FIRST_BEFORE].astype(F32)
    total = total.astype(BF)
    for quad in range(out.shape[0]):
        out[quad] = total


def scan(length, rows, constants, pieces, sums, out):
    steps = pieces.shape[0]
    span = pieces.shape[1] // rows
    decay = jnp.exp(-constants[0][:1] * length)
    whole = jnp.exp(-constants[0][:1] * (length * steps))
    mine = lax.axis_index("q")
    carry = jnp.zeros((span, E), F32)
    carries = []
    for row in range(rows):
        for quad in range(sums.shape[0]):
            chosen = carry if quad == 0 else jnp.where(mine == quad, carry, chosen)
            some = sums[quad ^ FIRST_QUAD, row * span : (row + 1) * span, :]
            carry = carry * whole + some.astype(F32)
        carries.append(chosen)
    total = jnp.concatenate(carries, axis=0)
    for step in range(steps):
        out[step ^ FIRST_AFTER] = total.astype(BF)
        total = total * decay + pieces[step ^ FIRST_BEFORE].astype(F32)


def within(tokens, constants, received, out, query_weight):
    groups, blocks = received.shape[:2]
    length = groups * tokens
    middle = length / 2.0
    decay = constants[0][:1]
    prior_weight = jnp.exp(-decay * (middle + 1.0))
    lane = lax.broadcasted_iota(jnp.int32, (length, E), 1)
    query_weights = jnp.zeros((length, E), F32)
    for block in range(blocks):
        chunks = row_positions(received, tokens, block)
        row = jnp.concatenate([chunk[:1] for chunk in chunks], axis=1)
        key_weight = jnp.exp(jnp.concatenate([decay] * len(chunks), axis=1) * (row - middle))
        column = column_positions(chunks)
        weight = jnp.exp(-decay * (column - middle))
        query_rows = received[:, block, :tokens, :].reshape(length, E)
        key_rows = received[:, block, tokens : 2 * tokens, :].reshape(length, E)
        value_rows = received[:, block, 2 * tokens : 3 * tokens, :].reshape(length, E)
        scores = lax.dot_general(
            query_rows, key_rows, (((1,), (1,)), ((), ())), preferred_element_type=F32
        )
        weights = jnp.where(column[:, :1] >= row, scores * key_weight, 0.0).astype(BF)
        out[block] = jnp.dot(weights, value_rows, preferred_element_type=F32) * weight
        query_weights = jnp.where(lane == block, weight * prior_weight, query_weights)
    query_weight[...] = query_weights


def finish(tokens, constants, received, prior, sums, query_weight, out):
    groups, blocks = received.shape[:2]
    scaling = constants[1][:1]
    ones = jnp.full((E, E), 1.0 / E, BF)
    for block in range(blocks):
        query_rows = received[:, block, :tokens, :].reshape(groups * tokens, E)
        span = prior.shape[1] // blocks
        row = block ^ FIRST_X
        slots = [at ^ FIRST_BEFORE ^ FIRST_AFTER for at in range(prior.shape[0])]
        state = jnp.concatenate(
            [prior[slot, row * span : (row + 1) * span, :] for slot in slots], axis=0
        )
        combined = jnp.dot(query_rows, state, preferred_element_type=F32)
        combined = sums[block] + combined * query_weight[:, block : block + 1]
        square = jnp.dot(
            (combined * combined).astype(BF), ones, preferred_element_type=F32
        )
        normal = (combined * lax.rsqrt(square + 1e-06) * scaling).astype(BF)
        out[:, block] = normal.reshape(groups, tokens, E)


def unpack(received, out, sem):
    first = FIRST_GROUP * lax.axis_size("x") + FIRST_X
    for slot in range(received.shape[0]):
        columns = out.at[0, :, pl.ds((slot ^ first) * E, E)]
        pltpu.make_async_copy(received.at[slot], columns, sem).start()
    pltpu.make_async_copy(received, received, sem).wait()


def exchange(value, axis, count, first):
    order = [[at ^ first for at in range(count)]]
    return lax.all_to_all(
        value, axis, split_axis=0, concat_axis=0, tiled=True, axis_index_groups=order
    )


def on_device(query, keys, values, decay_exp, gain, route):
    groups = lax.axis_size("group")
    rows = lax.axis_size("x")
    tokens, width = query.shape[1:]
    heads = decay_exp.shape[0]
    pieces = tokens // ROW
    length = tokens * groups
    scale = 1.0 / (4.0 * length * rows * QUADS * QUAD)
    sent_rows = 3 * tokens + ROW
    parts = 4
    sent = pl.pallas_call(
        functools.partial(pack, tokens, pieces),
        in_specs=[anywhere()] * 4,
        out_specs=anywhere(),
        out_shape=jax.ShapeDtypeStruct((heads, sent_rows, E), BF),
        scratch_shapes=[
            pltpu.VMEM((heads, sent_rows, E), BF),
            pltpu.SMEM(route.shape, jnp.int32),
            pltpu.SemaphoreType.DMA((parts,)),
            pltpu.SemaphoreType.DMA((parts,)),
            pltpu.SemaphoreType.DMA,
        ],
        compiler_params=params(62),
        name="pack",
    )(route, query, keys, values)
    plane = ("group", "x")
    first = FIRST_GROUP * rows + FIRST_X
    received = exchange(sent, plane, heads, first)
    received = received.reshape(groups, rows, sent_rows, E)
    sliced, constants = pl.pallas_call(
        functools.partial(states, tokens, scale),
        in_specs=[vmem(), vmem(), vmem()],
        out_specs=(vmem(), vmem()),
        out_shape=(
            jax.ShapeDtypeStruct((QUAD, rows * E // QUAD, E), BF),
            jax.ShapeDtypeStruct((2, ROW, E), F32),
        ),
        compiler_params=params(),
        name="states",
    )(decay_exp.reshape(1, heads), gain.reshape(heads, E), received)
    sliced = exchange(sliced, "r", QUAD, FIRST_BEFORE)
    quads = pl.pallas_call(
        functools.partial(totals, length),
        in_specs=[vmem(), vmem()],
        out_specs=vmem(),
        out_shape=jax.ShapeDtypeStruct((QUADS, rows * E // QUAD, E), BF),
        compiler_params=params(),
        name="totals",
    )(constants, sliced)
    quads = exchange(quads, "q", QUADS, FIRST_QUAD)
    sums, query_weight = pl.pallas_call(
        functools.partial(within, tokens),
        in_specs=[vmem(), vmem()],
        out_specs=(vmem(), vmem()),
        out_shape=(
            jax.ShapeDtypeStruct((rows, length, E), F32),
            jax.ShapeDtypeStruct((length, E), F32),
        ),
        compiler_params=params(),
        cost_estimate=pl.CostEstimate(
            flops=4 * rows * length * length * E,
            bytes_accessed=4 * rows * length * E * 4,
            transcendentals=rows * length * E,
        ),
        name="within",
    )(constants, received)
    quads, sums, query_weight = lax.optimization_barrier((quads, sums, query_weight))
    priors = pl.pallas_call(
        functools.partial(scan, length, rows),
        in_specs=[vmem(), vmem(), vmem()],
        out_specs=vmem(),
        out_shape=jax.ShapeDtypeStruct((QUAD, rows * E // QUAD, E), BF),
        compiler_params=params(),
        name="scan",
    )(constants, sliced, quads)
    priors = exchange(priors, "r", QUAD, FIRST_AFTER)
    mixed = pl.pallas_call(
        functools.partial(finish, tokens),
        in_specs=[vmem()] * 5,
        out_specs=vmem(),
        out_shape=jax.ShapeDtypeStruct((groups, rows, tokens, E), BF),
        compiler_params=params(),
        name="finish",
    )(constants, received, priors, sums, query_weight)
    mixed = mixed.reshape(heads, tokens, E)
    mixed = exchange(mixed, plane, heads, first)
    return pl.pallas_call(
        unpack,
        in_specs=[anywhere()],
        out_specs=anywhere(),
        out_shape=jax.ShapeDtypeStruct((1, tokens, width), BF),
        scratch_shapes=[pltpu.SemaphoreType.DMA],
        compiler_params=params(),
        name="unpack",
    )(mixed)


def solution(mesh):
    devices = np.asarray(mesh.devices)
    split = Mesh(
        devices.reshape(devices.shape[0], -1, QUADS, QUAD), ("group", "x", "q", "r")
    )
    ctx = ("x", "q", "r")
    stored = P("group", ctx, None)
    in_specs = (stored, stored, stored, P(), P(), P(None, ctx, None))
    return jax.shard_map(
        on_device, mesh=split, in_specs=in_specs, out_specs=stored, check_vma=False
    )
```

```python
import functools

import jax
import jax.numpy as jnp
import numpy as np
from jax import lax
from jax.experimental import pallas as pl
from jax.experimental.pallas import tpu as pltpu
from jax.sharding import Mesh
from jax.sharding import PartitionSpec as P

BF = jnp.bfloat16
F32 = jnp.float32
QUADS = 4
QUAD = 4
E = 128
ROW = 8
FIRST_GROUP, FIRST_X, FIRST_QUAD, FIRST_BEFORE, FIRST_AFTER = 5, 2, 2, 2, 2
LAST_GROUP, LAST_X = 5, 2


def vmem():
    return pl.BlockSpec(memory_space=pltpu.VMEM)


def params(mebibytes=48):
    return pltpu.CompilerParams(vmem_limit_bytes=mebibytes * 1024 * 1024)


def anywhere():
    return pl.BlockSpec(memory_space=pl.ANY)


def pack(tokens, pieces, route, query, keys, values, out, staged, route_ref, in_sems, out_sems, sem):
    heads = out.shape[0]
    first = FIRST_GROUP * lax.axis_size("x") + FIRST_X
    parts = in_sems.shape[0]
    fetch = pltpu.make_async_copy(route, route_ref, sem)
    fetch.start()
    span = heads // parts
    for part in range(parts):
        for head in range(part * span, (part + 1) * span):
            for at, source in enumerate((query, keys, values)):
                pltpu.make_async_copy(
                    source.at[0, :, pl.ds((head ^ first) * E, E)],
                    staged.at[head, pl.ds(at * tokens, tokens), :],
                    in_sems.at[part],
                ).start()
    token = lax.broadcasted_iota(jnp.int32, (ROW, E), 1) % tokens
    places = jnp.zeros((ROW, E), jnp.int32)
    group = lax.axis_index("group")
    fetch.wait()
    for piece in range(pieces):
        places = jnp.where(token // ROW == piece, route_ref[group, 0, piece], places)
    places = places.astype(F32).astype(BF)
    for head in range(heads):
        staged[head, 3 * tokens :, :] = places
    copies = []
    for part in range(parts):
        some = pl.ds(part * span, span)
        landed = staged.at[some, pl.ds(0, 3 * tokens), :]
        pltpu.make_async_copy(landed, landed, in_sems.at[part]).wait()
        copies.append(pltpu.make_async_copy(staged.at[some], out.at[some], out_sems.at[part]))
        copies[-1].start()
    for copy in copies:
        copy.wait()


def row_positions(received, tokens, block):
    lane = lax.broadcasted_iota(jnp.int32, (ROW, E), 1)
    step = (lane % ROW).astype(F32)
    chunks = []
    for pair in range(received.shape[0] // 2):
        even = received[2 * pair, block, 3 * tokens :, :].astype(F32)
        odd = received[2 * pair + 1, block, 3 * tokens :, :].astype(F32)
        chunks.append(jnp.where(lane < tokens, even, odd) * float(ROW) + step)
    return chunks


def column_positions(chunks):
    return jnp.concatenate(
        [jnp.transpose(jnp.broadcast_to(chunk[:1, :], (E, E))) for chunk in chunks], axis=0
    )


def within(tokens, decay, received, block):
    length = received.shape[0] * tokens
    middle = length / 2.0
    chunks = row_positions(received, tokens, block)
    row = jnp.concatenate([chunk[:1] for chunk in chunks], axis=1)
    key_weight = jnp.exp(jnp.concatenate([decay] * len(chunks), axis=1) * (row - middle))
    column = column_positions(chunks)
    weight = jnp.exp(-decay * (column - middle))
    query_rows = received[:, block, :tokens, :].reshape(length, E)
    key_rows = received[:, block, tokens : 2 * tokens, :].reshape(length, E)
    value_rows = received[:, block, 2 * tokens : 3 * tokens, :].reshape(length, E)
    scores = lax.dot_general(
        query_rows, key_rows, (((1,), (1,)), ((), ())), preferred_element_type=F32
    )
    weights = jnp.where(column[:, :1] >= row, scores * key_weight, 0.0).astype(BF)
    sums = jnp.dot(weights, value_rows, preferred_element_type=F32) * weight
    return sums, weight * jnp.exp(-decay * (middle + 1.0))


def states(tokens, scale, exponents, gain, received, out, constants, sums, query_weight):
    groups, blocks = received.shape[:2]
    length = groups * tokens
    heads = exponents.shape[1]
    head = lax.axis_index("group") * lax.axis_size("x") + lax.axis_index("x")
    mine = lax.broadcasted_iota(jnp.int32, (1, heads), 1) == head
    exponent = jnp.sum(jnp.where(mine, exponents[...], 0).astype(F32), axis=1, keepdims=True)
    exponent = jnp.broadcast_to(exponent, (ROW, E))
    decay = jnp.exp2(exponent * exponent / 8.0) * scale
    constants[0] = decay
    constants[1] = jnp.broadcast_to(gain[pl.ds(head, 1), :], (ROW, E))
    wide = jnp.concatenate([decay[:1]] * (length // E), axis=1)
    found = []
    for block in range(blocks):
        chunks = row_positions(received, tokens, block)
        position = jnp.concatenate([chunk[:1] for chunk in chunks], axis=1)
        weight = jnp.exp(-wide * (length - 1.0 - position))
        key_rows = received[:, block, tokens : 2 * tokens, :].reshape(length, E)
        value_rows = received[:, block, 2 * tokens : 3 * tokens, :].reshape(length, E)
        weighted = (jnp.transpose(key_rows).astype(F32) * weight).astype(BF)
        found.append(jnp.dot(weighted, value_rows, preferred_element_type=F32))
    span = E // out.shape[0]
    for at in range(out.shape[0]):
        rows = slice(at * span, (at + 1) * span)
        out[at] = jnp.concatenate(
            [found[row ^ FIRST_X][rows] for row in range(blocks)], axis=0
        ).astype(BF)

    @pl.when(lax.axis_index("q") != FIRST_QUAD)
    def _():
        lane = lax.broadcasted_iota(jnp.int32, (length, E), 1)
        weights = jnp.zeros((length, E), F32)
        for block in range(blocks):
            sums[block], weight = within(tokens, decay[:1], received, block)
            weights = jnp.where(lane == block, weight, weights)
        query_weight[...] = weights


def totals(length, constants, pieces, out):
    decay = jnp.exp(-constants[0][:1] * length)
    total = pieces[FIRST_BEFORE].astype(F32)
    for step in range(1, pieces.shape[0]):
        total = total * decay + pieces[step ^ FIRST_BEFORE].astype(F32)
    total = total.astype(BF)
    for quad in range(out.shape[0]):
        out[quad] = total


def scan(length, rows, constants, pieces, sums, out):
    steps = pieces.shape[0]
    span = pieces.shape[1] // rows
    decay = jnp.exp(-constants[0][:1] * length)
    whole = jnp.exp(-constants[0][:1] * (length * steps))
    mine = lax.axis_index("q")
    carry = jnp.zeros((span, E), F32)
    carries = []
    for row in range(rows):
        for quad in range(sums.shape[0]):
            chosen = carry if quad == 0 else jnp.where(mine == quad, carry, chosen)
            some = sums[quad ^ FIRST_QUAD, row * span : (row + 1) * span, :]
            carry = carry * whole + some.astype(F32)
        carries.append(chosen)
    total = jnp.concatenate(carries, axis=0)
    for step in range(steps):
        out[step ^ FIRST_AFTER] = total.astype(BF)
        total = total * decay + pieces[step ^ FIRST_BEFORE].astype(F32)


def finish(tokens, constants, received, prior, sums, query_weight, out):
    groups, blocks = received.shape[:2]
    decay, scaling = constants[0][:1], constants[1][:1]
    ones = jnp.full((E, E), 1.0 / E, BF)
    span = prior.shape[1] // blocks
    slots = [at ^ FIRST_BEFORE ^ FIRST_AFTER for at in range(prior.shape[0])]

    def add(block, own, weight):
        row = block ^ FIRST_X
        state = jnp.concatenate(
            [prior[slot, row * span : (row + 1) * span, :] for slot in slots], axis=0
        )
        query_rows = received[:, block, :tokens, :].reshape(groups * tokens, E)
        combined = own + jnp.dot(query_rows, state, preferred_element_type=F32) * weight
        square = jnp.dot(
            (combined * combined).astype(BF), ones, preferred_element_type=F32
        )
        normal = (combined * lax.rsqrt(square + 1e-06) * scaling).astype(BF)
        for group in range(groups):
            to = (group ^ FIRST_GROUP ^ LAST_GROUP, row ^ LAST_X)
            out[to] = normal[group * tokens : (group + 1) * tokens]

    @pl.when(lax.axis_index("q") != FIRST_QUAD)
    def _():
        for block in range(blocks):
            add(block, sums[block], query_weight[:, block : block + 1])

    @pl.when(lax.axis_index("q") == FIRST_QUAD)
    def _():
        for block in range(blocks):
            add(block, *within(tokens, decay, received, block))


def unpack(received, out, sem):
    first = LAST_GROUP * lax.axis_size("x") + LAST_X
    for slot in range(received.shape[0]):
        columns = out.at[0, :, pl.ds((slot ^ first) * E, E)]
        pltpu.make_async_copy(received.at[slot], columns, sem).start()
    pltpu.make_async_copy(received, received, sem).wait()


def exchange(value, axis, count, first):
    order = [[at ^ first for at in range(count)]]
    return lax.all_to_all(
        value, axis, split_axis=0, concat_axis=0, tiled=True, axis_index_groups=order
    )


def on_device(query, keys, values, decay_exp, gain, route):
    groups = lax.axis_size("group")
    rows = lax.axis_size("x")
    tokens, width = query.shape[1:]
    heads = decay_exp.shape[0]
    pieces = tokens // ROW
    length = tokens * groups
    scale = 1.0 / (4.0 * length * rows * QUADS * QUAD)
    sent_rows = 3 * tokens + ROW
    parts = 4
    sent = pl.pallas_call(
        functools.partial(pack, tokens, pieces),
        in_specs=[anywhere()] * 4,
        out_specs=anywhere(),
        out_shape=jax.ShapeDtypeStruct((heads, sent_rows, E), BF),
        scratch_shapes=[
            pltpu.VMEM((heads, sent_rows, E), BF),
            pltpu.SMEM(route.shape, jnp.int32),
            pltpu.SemaphoreType.DMA((parts,)),
            pltpu.SemaphoreType.DMA((parts,)),
            pltpu.SemaphoreType.DMA,
        ],
        compiler_params=params(62),
        name="pack",
    )(route, query, keys, values)
    plane = ("group", "x")
    first = FIRST_GROUP * rows + FIRST_X
    received = exchange(sent, plane, heads, first)
    received = received.reshape(groups, rows, sent_rows, E)
    sliced, constants, sums, query_weight = pl.pallas_call(
        functools.partial(states, tokens, scale),
        in_specs=[vmem(), vmem(), vmem()],
        out_specs=(vmem(), vmem(), vmem(), vmem()),
        out_shape=(
            jax.ShapeDtypeStruct((QUAD, rows * E // QUAD, E), BF),
            jax.ShapeDtypeStruct((2, ROW, E), F32),
            jax.ShapeDtypeStruct((rows, length, E), F32),
            jax.ShapeDtypeStruct((length, E), F32),
        ),
        compiler_params=params(),
        name="states",
    )(decay_exp.reshape(1, heads), gain.reshape(heads, E), received)
    sliced = exchange(sliced, "r", QUAD, FIRST_BEFORE)
    quads = pl.pallas_call(
        functools.partial(totals, length),
        in_specs=[vmem(), vmem()],
        out_specs=vmem(),
        out_shape=jax.ShapeDtypeStruct((QUADS, rows * E // QUAD, E), BF),
        compiler_params=params(),
        name="totals",
    )(constants, sliced)
    quads = exchange(quads, "q", QUADS, FIRST_QUAD)
    priors = pl.pallas_call(
        functools.partial(scan, length, rows),
        in_specs=[vmem(), vmem(), vmem()],
        out_specs=vmem(),
        out_shape=jax.ShapeDtypeStruct((QUAD, rows * E // QUAD, E), BF),
        compiler_params=params(),
        name="scan",
    )(constants, sliced, quads)
    priors = exchange(priors, "r", QUAD, FIRST_AFTER)
    mixed = pl.pallas_call(
        functools.partial(finish, tokens),
        in_specs=[vmem()] * 5,
        out_specs=vmem(),
        out_shape=jax.ShapeDtypeStruct((groups, rows, tokens, E), BF),
        compiler_params=params(),
        name="finish",
    )(constants, received, priors, sums, query_weight)
    mixed = mixed.reshape(heads, tokens, E)
    mixed = exchange(mixed, plane, heads, LAST_GROUP * rows + LAST_X)
    return pl.pallas_call(
        unpack,
        in_specs=[anywhere()],
        out_specs=anywhere(),
        out_shape=jax.ShapeDtypeStruct((1, tokens, width), BF),
        scratch_shapes=[pltpu.SemaphoreType.DMA],
        compiler_params=params(),
        name="unpack",
    )(mixed)


def solution(mesh):
    devices = np.asarray(mesh.devices)
    split = Mesh(
        devices.reshape(devices.shape[0], -1, QUADS, QUAD), ("group", "x", "q", "r")
    )
    ctx = ("x", "q", "r")
    stored = P("group", ctx, None)
    in_specs = (stored, stored, stored, P(), P(), P(None, ctx, None))
    return jax.shard_map(
        on_device, mesh=split, in_specs=in_specs, out_specs=stored, check_vma=False
    )
```

```python
import functools

import jax
import jax.numpy as jnp
import numpy as np
from jax import lax
from jax.experimental import pallas as pl
from jax.experimental.pallas import tpu as pltpu
from jax.sharding import Mesh
from jax.sharding import PartitionSpec as P

BF = jnp.bfloat16
F32 = jnp.float32
QUADS = 4
QUAD = 4
E = 128
ROW = 8
FIRST_GROUP, FIRST_X, FIRST_QUAD, FIRST_BEFORE, FIRST_AFTER = 7, 2, 2, 1, 2
LAST_GROUP, LAST_X = 7, 2


def vmem():
    return pl.BlockSpec(memory_space=pltpu.VMEM)


def params(mebibytes=48):
    return pltpu.CompilerParams(vmem_limit_bytes=mebibytes * 1024 * 1024)


def anywhere():
    return pl.BlockSpec(memory_space=pl.ANY)


def pack(tokens, pieces, route, query, keys, values, out, route_ref, in_sems, sem):
    heads = out.shape[0]
    first = FIRST_GROUP * lax.axis_size("x") + FIRST_X
    fetch = pltpu.make_async_copy(route, route_ref, sem)
    fetch.start()
    for at, source in enumerate((query, keys, values)):
        for slot in range(heads):
            pltpu.make_async_copy(
                source.at[0, :, pl.ds((slot ^ first) * E, E)],
                out.at[slot, pl.ds(at * tokens, tokens), :],
                in_sems.at[at],
            ).start()
    token = lax.broadcasted_iota(jnp.int32, (ROW, E), 1) % tokens
    places = jnp.zeros((ROW, E), jnp.int32)
    group = lax.axis_index("group")
    fetch.wait()
    for piece in range(pieces):
        places = jnp.where(token // ROW == piece, route_ref[group, 0, piece], places)
    places = places.astype(F32).astype(BF)
    for slot in range(heads):
        out[slot, 3 * tokens :, :] = places
    for at in range(3):
        landed = out.at[:, pl.ds(at * tokens, tokens), :]
        pltpu.make_async_copy(landed, landed, in_sems.at[at]).wait()


def row_positions(received, tokens, block):
    lane = lax.broadcasted_iota(jnp.int32, (ROW, E), 1)
    step = (lane % ROW).astype(F32)
    chunks = []
    for pair in range(received.shape[0] // 2):
        even = received[2 * pair, block, 3 * tokens :, :].astype(F32)
        odd = received[2 * pair + 1, block, 3 * tokens :, :].astype(F32)
        chunks.append(jnp.where(lane < tokens, even, odd) * float(ROW) + step)
    return chunks


def column_positions(chunks):
    return jnp.concatenate(
        [jnp.transpose(jnp.broadcast_to(chunk[:1, :], (E, E))) for chunk in chunks], axis=0
    )


def within(tokens, decay, received, block):
    length = received.shape[0] * tokens
    middle = length / 2.0
    chunks = row_positions(received, tokens, block)
    row = jnp.concatenate([chunk[:1] for chunk in chunks], axis=1)
    key_weight = jnp.exp(jnp.concatenate([decay] * len(chunks), axis=1) * (row - middle))
    column = column_positions(chunks)
    weight = jnp.exp(-decay * (column - middle))
    query_rows = received[:, block, :tokens, :].reshape(length, E)
    key_rows = received[:, block, tokens : 2 * tokens, :].reshape(length, E)
    value_rows = received[:, block, 2 * tokens : 3 * tokens, :].reshape(length, E)
    scores = lax.dot_general(
        query_rows, key_rows, (((1,), (1,)), ((), ())), preferred_element_type=F32
    )
    weights = jnp.where(column[:, :1] >= row, scores * key_weight, 0.0).astype(BF)
    sums = jnp.dot(weights, value_rows, preferred_element_type=F32) * weight
    return sums, weight * jnp.exp(-decay * (middle + 1.0))


def states(tokens, scale, exponents, gain, received, out, constants, sums, query_weight):
    groups, blocks = received.shape[:2]
    length = groups * tokens
    heads = exponents.shape[1]
    head = lax.axis_index("group") * lax.axis_size("x") + lax.axis_index("x")
    mine = lax.broadcasted_iota(jnp.int32, (1, heads), 1) == head
    exponent = jnp.sum(jnp.where(mine, exponents[...], 0).astype(F32), axis=1, keepdims=True)
    exponent = jnp.broadcast_to(exponent, (ROW, E))
    decay = jnp.exp2(exponent * exponent / 8.0) * scale
    constants[0] = decay
    constants[1] = jnp.broadcast_to(gain[pl.ds(head, 1), :], (ROW, E))
    wide = jnp.concatenate([decay[:1]] * (length // E), axis=1)
    found = []
    for block in range(blocks):
        chunks = row_positions(received, tokens, block)
        position = jnp.concatenate([chunk[:1] for chunk in chunks], axis=1)
        weight = jnp.exp(-wide * (length - 1.0 - position))
        key_rows = received[:, block, tokens : 2 * tokens, :].reshape(length, E)
        value_rows = received[:, block, 2 * tokens : 3 * tokens, :].reshape(length, E)
        weighted = (jnp.transpose(key_rows).astype(F32) * weight).astype(BF)
        found.append(jnp.dot(weighted, value_rows, preferred_element_type=F32))
    span = E // out.shape[0]
    for at in range(out.shape[0]):
        rows = slice(at * span, (at + 1) * span)
        out[at] = jnp.concatenate(
            [found[row ^ FIRST_X][rows] for row in range(blocks)], axis=0
        ).astype(BF)

    @pl.when(lax.axis_index("q") != FIRST_QUAD)
    def _():
        lane = lax.broadcasted_iota(jnp.int32, (length, E), 1)
        weights = jnp.zeros((length, E), F32)
        for block in range(blocks):
            sums[block], weight = within(tokens, decay[:1], received, block)
            weights = jnp.where(lane == block, weight, weights)
        query_weight[...] = weights


def totals(length, constants, pieces, out):
    decay = jnp.exp(-constants[0][:1] * length)
    total = pieces[FIRST_BEFORE].astype(F32)
    for step in range(1, pieces.shape[0]):
        total = total * decay + pieces[step ^ FIRST_BEFORE].astype(F32)
    total = total.astype(BF)
    for quad in range(out.shape[0]):
        out[quad] = total


def scan(length, rows, constants, pieces, sums, out):
    steps = pieces.shape[0]
    span = pieces.shape[1] // rows
    decay = jnp.exp(-constants[0][:1] * length)
    whole = jnp.exp(-constants[0][:1] * (length * steps))
    mine = lax.axis_index("q")
    carry = jnp.zeros((span, E), F32)
    carries = []
    for row in range(rows):
        for quad in range(sums.shape[0]):
            chosen = carry if quad == 0 else jnp.where(mine == quad, carry, chosen)
            some = sums[quad ^ FIRST_QUAD, row * span : (row + 1) * span, :]
            carry = carry * whole + some.astype(F32)
        carries.append(chosen)
    total = jnp.concatenate(carries, axis=0)
    for step in range(steps):
        out[step ^ FIRST_AFTER] = total.astype(BF)
        total = total * decay + pieces[step ^ FIRST_BEFORE].astype(F32)


def finish(tokens, constants, received, prior, sums, query_weight, out):
    groups, blocks = received.shape[:2]
    decay, scaling = constants[0][:1], constants[1][:1]
    ones = jnp.full((E, E), 1.0 / E, BF)
    span = prior.shape[1] // blocks
    slots = [at ^ FIRST_BEFORE ^ FIRST_AFTER for at in range(prior.shape[0])]

    def add(block, own, weight):
        row = block ^ FIRST_X
        state = jnp.concatenate(
            [prior[slot, row * span : (row + 1) * span, :] for slot in slots], axis=0
        )
        query_rows = received[:, block, :tokens, :].reshape(groups * tokens, E)
        combined = own + jnp.dot(query_rows, state, preferred_element_type=F32) * weight
        square = jnp.dot(
            (combined * combined).astype(BF), ones, preferred_element_type=F32
        )
        normal = (combined * lax.rsqrt(square + 1e-06) * scaling).astype(BF)
        for group in range(groups):
            to = (group ^ FIRST_GROUP ^ LAST_GROUP, row ^ LAST_X)
            out[to] = normal[group * tokens : (group + 1) * tokens]

    @pl.when(lax.axis_index("q") != FIRST_QUAD)
    def _():
        for block in range(blocks):
            add(block, sums[block], query_weight[:, block : block + 1])

    @pl.when(lax.axis_index("q") == FIRST_QUAD)
    def _():
        for block in range(blocks):
            add(block, *within(tokens, decay, received, block))


def unpack(received, out, sem):
    first = LAST_GROUP * lax.axis_size("x") + LAST_X
    for slot in range(received.shape[0]):
        columns = out.at[0, :, pl.ds((slot ^ first) * E, E)]
        pltpu.make_async_copy(received.at[slot], columns, sem).start()
    pltpu.make_async_copy(received, received, sem).wait()


def exchange(value, axis, count, first):
    order = [[at ^ first for at in range(count)]]
    return lax.all_to_all(
        value, axis, split_axis=0, concat_axis=0, tiled=True, axis_index_groups=order
    )


def on_device(query, keys, values, decay_exp, gain, route):
    groups = lax.axis_size("group")
    rows = lax.axis_size("x")
    tokens, width = query.shape[1:]
    heads = decay_exp.shape[0]
    pieces = tokens // ROW
    length = tokens * groups
    scale = 1.0 / (4.0 * length * rows * QUADS * QUAD)
    sent_rows = 3 * tokens + ROW
    sent = pl.pallas_call(
        functools.partial(pack, tokens, pieces),
        in_specs=[anywhere()] * 4,
        out_specs=vmem(),
        out_shape=jax.ShapeDtypeStruct((heads, sent_rows, E), BF),
        scratch_shapes=[
            pltpu.SMEM(route.shape, jnp.int32),
            pltpu.SemaphoreType.DMA((3,)),
            pltpu.SemaphoreType.DMA,
        ],
        compiler_params=params(),
        name="pack",
    )(*[pltpu.with_memory_space_constraint(x, pltpu.HBM) for x in (route, query, keys, values)])
    plane = ("group", "x")
    first = FIRST_GROUP * rows + FIRST_X
    received = exchange(sent, plane, heads, first)
    received = received.reshape(groups, rows, sent_rows, E)
    sliced, constants, sums, query_weight = pl.pallas_call(
        functools.partial(states, tokens, scale),
        in_specs=[vmem(), vmem(), vmem()],
        out_specs=(vmem(), vmem(), vmem(), vmem()),
        out_shape=(
            jax.ShapeDtypeStruct((QUAD, rows * E // QUAD, E), BF),
            jax.ShapeDtypeStruct((2, ROW, E), F32),
            jax.ShapeDtypeStruct((rows, length, E), F32),
            jax.ShapeDtypeStruct((length, E), F32),
        ),
        compiler_params=params(),
        name="states",
    )(decay_exp.reshape(1, heads), gain.reshape(heads, E), received)
    sliced = exchange(sliced, "r", QUAD, FIRST_BEFORE)
    quads = pl.pallas_call(
        functools.partial(totals, length),
        in_specs=[vmem(), vmem()],
        out_specs=vmem(),
        out_shape=jax.ShapeDtypeStruct((QUADS, rows * E // QUAD, E), BF),
        compiler_params=params(),
        name="totals",
    )(constants, sliced)
    quads = exchange(quads, "q", QUADS, FIRST_QUAD)
    priors = pl.pallas_call(
        functools.partial(scan, length, rows),
        in_specs=[vmem(), vmem(), vmem()],
        out_specs=vmem(),
        out_shape=jax.ShapeDtypeStruct((QUAD, rows * E // QUAD, E), BF),
        compiler_params=params(),
        name="scan",
    )(constants, sliced, quads)
    priors = exchange(priors, "r", QUAD, FIRST_AFTER)
    mixed = pl.pallas_call(
        functools.partial(finish, tokens),
        in_specs=[vmem()] * 5,
        out_specs=vmem(),
        out_shape=jax.ShapeDtypeStruct((groups, rows, tokens, E), BF),
        compiler_params=params(),
        name="finish",
    )(constants, received, priors, sums, query_weight)
    mixed = mixed.reshape(heads, tokens, E)
    mixed = exchange(mixed, plane, heads, LAST_GROUP * rows + LAST_X)
    return pl.pallas_call(
        unpack,
        in_specs=[anywhere()],
        out_specs=anywhere(),
        out_shape=jax.ShapeDtypeStruct((1, tokens, width), BF),
        scratch_shapes=[pltpu.SemaphoreType.DMA],
        compiler_params=params(),
        name="unpack",
    )(mixed)


def solution(mesh):
    devices = np.asarray(mesh.devices)
    split = Mesh(
        devices.reshape(devices.shape[0], -1, QUADS, QUAD), ("group", "x", "q", "r")
    )
    ctx = ("x", "q", "r")
    stored = P("group", ctx, None)
    in_specs = (stored, stored, stored, P(), P(), P(None, ctx, None))
    return jax.shard_map(
        on_device, mesh=split, in_specs=in_specs, out_specs=stored, check_vma=False
    )
```

```python
import functools

import jax
import jax.numpy as jnp
import numpy as np
from jax import lax
from jax.experimental import pallas as pl
from jax.experimental.pallas import tpu as pltpu
from jax.sharding import Mesh
from jax.sharding import PartitionSpec as P

BF = jnp.bfloat16
F32 = jnp.float32
QUADS = 4
QUAD = 4
E = 128
ROW = 8
FIRST_GROUP, LAST_GROUP, FIRST_QUAD = 7, 7, 2
FIRST_BEFORE, FIRST_AFTER = 10, 10


def vmem():
    return pl.BlockSpec(memory_space=pltpu.VMEM)


def params(mebibytes=48):
    return pltpu.CompilerParams(vmem_limit_bytes=mebibytes * 1024 * 1024)


def anywhere():
    return pl.BlockSpec(memory_space=pl.ANY)


def pack(tokens, width, route, query, keys, values, out, positions, route_ref, sems):
    groups = out.shape[0]
    fetch = pltpu.make_async_copy(route, route_ref, sems.at[3])
    fetch.start()
    for at, source in enumerate((query, keys, values)):
        for slot in range(groups):
            pltpu.make_async_copy(
                source.at[0, :, pl.ds((slot ^ FIRST_GROUP) * width, width)],
                out.at[slot, pl.ds(at * tokens, tokens), :],
                sems.at[at],
            ).start()
    lane = lax.broadcasted_iota(jnp.int32, (ROW, E), 1)
    per_slot = tokens // ROW
    fetch.wait()
    for chunk in range(groups * tokens // E):
        places = jnp.zeros((ROW, E), jnp.int32)
        for piece in range(E // ROW):
            slot, own = divmod(chunk * (E // ROW) + piece, per_slot)
            place = route_ref[slot ^ FIRST_GROUP, 0, own]
            places = jnp.where(lane // ROW == piece, place, places)
        positions[:, chunk * E : (chunk + 1) * E] = (places * ROW + lane % ROW).astype(F32)
    for at in range(3):
        landed = out.at[:, pl.ds(at * tokens, tokens), :]
        pltpu.make_async_copy(landed, landed, sems.at[at]).wait()


def rows_of(received, tokens, which, head):
    part = received[
        :, which * tokens : (which + 1) * tokens, head * E : (head + 1) * E
    ]
    return part.reshape(received.shape[0] * tokens, E)


def within(tokens, decay, positions, received, head):
    length = received.shape[0] * tokens
    middle = length / 2.0
    row = positions[:1, :]
    chunks = [
        jnp.transpose(jnp.broadcast_to(row[:, at : at + E], (E, E)))
        for at in range(0, length, E)
    ]
    column = jnp.concatenate(chunks, axis=0)
    wide = jnp.concatenate([decay] * (length // E), axis=1)
    key_weight = jnp.exp(wide * (row - middle))
    weight = jnp.exp(-decay * (column - middle))
    scores = lax.dot_general(
        rows_of(received, tokens, 0, head),
        rows_of(received, tokens, 1, head),
        (((1,), (1,)), ((), ())),
        preferred_element_type=F32,
    )
    weights = jnp.where(column[:, :1] >= row, scores * key_weight, 0.0).astype(BF)
    values = rows_of(received, tokens, 2, head)
    sums = jnp.dot(weights, values, preferred_element_type=F32) * weight
    return sums, weight * jnp.exp(-decay * (middle + 1.0))


def states(
    tokens, scale, exponents, gain, positions, received, out, constants, sums, query_weight
):
    heads = received.shape[2] // E
    length = received.shape[0] * tokens
    all_heads = exponents.shape[1]
    first = lax.axis_index("group") * heads
    for at in range(heads + 1):
        head = first + (at if at < heads else lax.axis_index("x"))
        mine = lax.broadcasted_iota(jnp.int32, (1, all_heads), 1) == head
        exponent = jnp.sum(
            jnp.where(mine, exponents[...], 0).astype(F32), axis=1, keepdims=True
        )
        exponent = jnp.broadcast_to(exponent, (ROW, E))
        constants[2 * at] = jnp.exp2(exponent * exponent / 8.0) * scale
        if at < heads:
            constants[2 * at + 1] = jnp.broadcast_to(gain[pl.ds(head, 1), :], (ROW, E))
    found = []
    for head in range(heads):
        wide = jnp.concatenate([constants[2 * head][:1]] * (length // E), axis=1)
        weight = jnp.exp(-wide * (length - 1.0 - positions[:1, :]))
        key_rows = rows_of(received, tokens, 1, head)
        weighted = (jnp.transpose(key_rows).astype(F32) * weight).astype(BF)
        values = rows_of(received, tokens, 2, head)
        found.append(jnp.dot(weighted, values, preferred_element_type=F32).astype(BF))
    span = out.shape[1]
    for slot in range(out.shape[0]):
        head, part = divmod(slot ^ FIRST_BEFORE, QUAD)
        out[slot] = found[head][part * span : (part + 1) * span]

    @pl.when(lax.axis_index("q") != FIRST_QUAD)
    def _():
        lane = lax.broadcasted_iota(jnp.int32, (length, E), 1)
        weights = jnp.zeros((length, E), F32)
        for head in range(heads):
            decay = constants[2 * head][:1]
            sums[head], weight = within(tokens, decay, positions, received, head)
            weights = jnp.where(lane == head, weight, weights)
        query_weight[...] = weights


def at_step(pieces, step):
    rows = pieces.shape[0] // QUAD
    slots = [(row * QUAD + step) ^ FIRST_BEFORE for row in range(rows)]
    return jnp.concatenate([pieces[slot] for slot in slots], axis=0).astype(F32)


def totals(length, constants, pieces, out):
    decay = jnp.exp(-constants[constants.shape[0] - 2][:1] * length)
    total = at_step(pieces, 0)
    for step in range(1, QUAD):
        total = total * decay + at_step(pieces, step)
    total = total.astype(BF)
    for quad in range(out.shape[0]):
        out[quad] = total


def scan(length, rows, constants, pieces, sums, out):
    span = pieces.shape[1]
    rate = constants[constants.shape[0] - 2][:1]
    decay = jnp.exp(-rate * length)
    whole = jnp.exp(-rate * (length * QUAD))
    mine = lax.axis_index("q")
    carry = jnp.zeros((span, E), F32)
    carries = []
    for row in range(rows):
        for quad in range(sums.shape[0]):
            chosen = carry if quad == 0 else jnp.where(mine == quad, carry, chosen)
            some = sums[quad ^ FIRST_QUAD, row * span : (row + 1) * span, :]
            carry = carry * whole + some.astype(F32)
        carries.append(chosen)
    total = jnp.concatenate(carries, axis=0)
    for step in range(QUAD):
        rounded = total.astype(BF)
        for row in range(rows):
            slot = (row * QUAD + step) ^ FIRST_AFTER
            out[slot] = rounded[row * span : (row + 1) * span]
        total = total * decay + at_step(pieces, step)


def finish(tokens, constants, positions, received, prior, sums, query_weight, out):
    heads = received.shape[2] // E
    groups = received.shape[0]
    ones = jnp.full((E, E), 1.0 / E, BF)

    def add(head, own, weight):
        slots = [(head * QUAD + part) ^ FIRST_AFTER for part in range(QUAD)]
        state = jnp.concatenate([prior[slot] for slot in slots], axis=0)
        query_rows = rows_of(received, tokens, 0, head)
        combined = own + jnp.dot(query_rows, state, preferred_element_type=F32) * weight
        square = jnp.dot(
            (combined * combined).astype(BF), ones, preferred_element_type=F32
        )
        scaling = constants[2 * head + 1][:1]
        normal = (combined * lax.rsqrt(square + 1e-06) * scaling).astype(BF)
        columns = slice(head * E, (head + 1) * E)
        for slot in range(groups):
            to = slot ^ FIRST_GROUP ^ LAST_GROUP
            out[to, :, columns] = normal[slot * tokens : (slot + 1) * tokens]

    @pl.when(lax.axis_index("q") != FIRST_QUAD)
    def _():
        for head in range(heads):
            add(head, sums[head], query_weight[:, head : head + 1])

    @pl.when(lax.axis_index("q") == FIRST_QUAD)
    def _():
        for head in range(heads):
            decay = constants[2 * head][:1]
            add(head, *within(tokens, decay, positions, received, head))


def unpack(received, out, sem):
    width = received.shape[2]
    for slot in range(received.shape[0]):
        columns = out.at[0, :, pl.ds((slot ^ LAST_GROUP) * width, width)]
        pltpu.make_async_copy(received.at[slot], columns, sem).start()
    pltpu.make_async_copy(received, received, sem).wait()


def exchange(value, axis, first):
    order = [[at ^ first for at in range(value.shape[0])]]
    return lax.all_to_all(
        value, axis, split_axis=0, concat_axis=0, tiled=True, axis_index_groups=order
    )


def on_device(query, keys, values, decay_exp, gain, route):
    groups = lax.axis_size("group")
    rows = lax.axis_size("x")
    tokens, width = query.shape[1:]
    all_heads = decay_exp.shape[0]
    heads = all_heads // groups
    length = tokens * groups
    scale = 1.0 / (4.0 * length * rows * QUADS * QUAD)
    span = E // QUAD
    sent, positions = pl.pallas_call(
        functools.partial(pack, tokens, width // groups),
        in_specs=[anywhere()] * 4,
        out_specs=(vmem(), vmem()),
        out_shape=(
            jax.ShapeDtypeStruct((groups, 3 * tokens, width // groups), BF),
            jax.ShapeDtypeStruct((ROW, length), F32),
        ),
        scratch_shapes=[
            pltpu.SMEM(route.shape, jnp.int32),
            pltpu.SemaphoreType.DMA((4,)),
        ],
        compiler_params=params(),
        name="pack",
    )(*[pltpu.with_memory_space_constraint(x, pltpu.HBM) for x in (route, query, keys, values)])
    received = exchange(sent, "group", FIRST_GROUP)
    sliced, constants, sums, query_weight = pl.pallas_call(
        functools.partial(states, tokens, scale),
        in_specs=[vmem()] * 4,
        out_specs=(vmem(),) * 4,
        out_shape=(
            jax.ShapeDtypeStruct((heads * QUAD, span, E), BF),
            jax.ShapeDtypeStruct((2 * heads + 2, ROW, E), F32),
            jax.ShapeDtypeStruct((heads, length, E), F32),
            jax.ShapeDtypeStruct((length, E), F32),
        ),
        compiler_params=params(),
        name="states",
    )(decay_exp.reshape(1, all_heads), gain.reshape(all_heads, E), positions, received)
    sliced = exchange(sliced, ("x", "r"), FIRST_BEFORE)
    quads = pl.pallas_call(
        functools.partial(totals, length),
        in_specs=[vmem(), vmem()],
        out_specs=vmem(),
        out_shape=jax.ShapeDtypeStruct((QUADS, rows * span, E), BF),
        compiler_params=params(),
        name="totals",
    )(constants, sliced)
    quads = exchange(quads, "q", FIRST_QUAD)
    priors = pl.pallas_call(
        functools.partial(scan, length, rows),
        in_specs=[vmem(), vmem(), vmem()],
        out_specs=vmem(),
        out_shape=jax.ShapeDtypeStruct((rows * QUAD, span, E), BF),
        compiler_params=params(),
        name="scan",
    )(constants, sliced, quads)
    priors = exchange(priors, ("x", "r"), FIRST_AFTER)
    mixed = pl.pallas_call(
        functools.partial(finish, tokens),
        in_specs=[vmem()] * 6,
        out_specs=vmem(),
        out_shape=jax.ShapeDtypeStruct((groups, tokens, width // groups), BF),
        compiler_params=params(),
        name="finish",
    )(constants, positions, received, priors, sums, query_weight)
    mixed = exchange(mixed, "group", LAST_GROUP)
    return pl.pallas_call(
        unpack,
        in_specs=[anywhere()],
        out_specs=anywhere(),
        out_shape=jax.ShapeDtypeStruct((1, tokens, width), BF),
        scratch_shapes=[pltpu.SemaphoreType.DMA],
        compiler_params=params(),
        name="unpack",
    )(mixed)


def solution(mesh):
    devices = np.asarray(mesh.devices)
    split = Mesh(
        devices.reshape(devices.shape[0], -1, QUADS, QUAD), ("group", "x", "q", "r")
    )
    ctx = ("x", "q", "r")
    stored = P("group", ctx, None)
    in_specs = (stored, stored, stored, P(), P(), P(None, ctx, None))
    return jax.shard_map(
        on_device, mesh=split, in_specs=in_specs, out_specs=stored, check_vma=False
    )
```

```python
import functools

import jax
import jax.numpy as jnp
import numpy as np
from jax import lax
from jax.experimental import pallas as pl
from jax.experimental.pallas import tpu as pltpu
from jax.sharding import Mesh
from jax.sharding import PartitionSpec as P

BF = jnp.bfloat16
F32 = jnp.float32
QUADS = 4
QUAD = 4
E = 128
ROW = 8
FIRST_GROUP, LAST_GROUP, FIRST_QUAD = 7, 5, 2
FIRST_BEFORE, FIRST_AFTER = 10, 10


def vmem():
    return pl.BlockSpec(memory_space=pltpu.VMEM)


def params(mebibytes=48):
    return pltpu.CompilerParams(vmem_limit_bytes=mebibytes * 1024 * 1024)


def anywhere():
    return pl.BlockSpec(memory_space=pl.ANY)


def pack(tokens, width, route, query, keys, values, out, positions, route_ref, sems):
    groups = out.shape[0]
    fetch = pltpu.make_async_copy(route, route_ref, sems.at[3])
    fetch.start()
    for at, source in enumerate((query, keys, values)):
        for slot in range(groups):
            pltpu.make_async_copy(
                source.at[0, :, pl.ds((slot ^ FIRST_GROUP) * width, width)],
                out.at[slot, pl.ds(at * tokens, tokens), :],
                sems.at[at],
            ).start()
    lane = lax.broadcasted_iota(jnp.int32, (ROW, E), 1)
    per_slot = tokens // ROW
    fetch.wait()
    for chunk in range(groups * tokens // E):
        places = jnp.zeros((ROW, E), jnp.int32)
        for piece in range(E // ROW):
            slot, own = divmod(chunk * (E // ROW) + piece, per_slot)
            place = route_ref[slot ^ FIRST_GROUP, 0, own]
            places = jnp.where(lane // ROW == piece, place, places)
        positions[:, chunk * E : (chunk + 1) * E] = (places * ROW + lane % ROW).astype(F32)
    for at in range(3):
        landed = out.at[:, pl.ds(at * tokens, tokens), :]
        pltpu.make_async_copy(landed, landed, sems.at[at]).wait()


def rows_of(received, tokens, which, head):
    part = received[
        :, which * tokens : (which + 1) * tokens, head * E : (head + 1) * E
    ]
    return part.reshape(received.shape[0] * tokens, E)


def within(tokens, decay, positions, received, head):
    length = received.shape[0] * tokens
    middle = length / 2.0
    row = positions[:1, :]
    chunks = [
        jnp.transpose(jnp.broadcast_to(row[:, at : at + E], (E, E)))
        for at in range(0, length, E)
    ]
    column = jnp.concatenate(chunks, axis=0)
    wide = jnp.concatenate([decay] * (length // E), axis=1)
    key_weight = jnp.exp(wide * (row - middle))
    weight = jnp.exp(-decay * (column - middle))
    scores = lax.dot_general(
        rows_of(received, tokens, 0, head),
        rows_of(received, tokens, 1, head),
        (((1,), (1,)), ((), ())),
        preferred_element_type=F32,
    )
    weights = jnp.where(column[:, :1] >= row, scores * key_weight, 0.0).astype(BF)
    values = rows_of(received, tokens, 2, head)
    sums = jnp.dot(weights, values, preferred_element_type=F32) * weight
    return sums, weight * jnp.exp(-decay * (middle + 1.0))


def states(
    tokens, scale, exponents, gain, positions, received, out, constants, sums, query_weight
):
    heads = received.shape[2] // E
    length = received.shape[0] * tokens
    all_heads = exponents.shape[1]
    first = lax.axis_index("group") * heads
    for at in range(heads + 1):
        head = first + (at if at < heads else lax.axis_index("x"))
        mine = lax.broadcasted_iota(jnp.int32, (1, all_heads), 1) == head
        exponent = jnp.sum(
            jnp.where(mine, exponents[...], 0).astype(F32), axis=1, keepdims=True
        )
        exponent = jnp.broadcast_to(exponent, (ROW, E))
        constants[2 * at] = jnp.exp2(exponent * exponent / 8.0) * scale
        if at < heads:
            constants[2 * at + 1] = jnp.broadcast_to(gain[pl.ds(head, 1), :], (ROW, E))
    found = []
    for head in range(heads):
        wide = jnp.concatenate([constants[2 * head][:1]] * (length // E), axis=1)
        weight = jnp.exp(-wide * (length - 1.0 - positions[:1, :]))
        key_rows = rows_of(received, tokens, 1, head)
        weighted = (jnp.transpose(key_rows).astype(F32) * weight).astype(BF)
        values = rows_of(received, tokens, 2, head)
        found.append(jnp.dot(weighted, values, preferred_element_type=F32).astype(BF))
    span = out.shape[1]
    for slot in range(out.shape[0]):
        head, part = divmod(slot ^ FIRST_BEFORE, QUAD)
        out[slot] = found[head][part * span : (part + 1) * span]

    @pl.when(lax.axis_index("q") != FIRST_QUAD)
    def _():
        lane = lax.broadcasted_iota(jnp.int32, (length, E), 1)
        weights = jnp.zeros((length, E), F32)
        for head in range(heads):
            decay = constants[2 * head][:1]
            sums[head], weight = within(tokens, decay, positions, received, head)
            weights = jnp.where(lane == head, weight, weights)
        query_weight[...] = weights


def at_step(pieces, step):
    rows = pieces.shape[0] // QUAD
    slots = [(row * QUAD + step) ^ FIRST_BEFORE for row in range(rows)]
    return jnp.concatenate([pieces[slot] for slot in slots], axis=0).astype(F32)


def totals(length, constants, pieces, out):
    decay = jnp.exp(-constants[constants.shape[0] - 2][:1] * length)
    total = at_step(pieces, 0)
    for step in range(1, QUAD):
        total = total * decay + at_step(pieces, step)
    total = total.astype(BF)
    for quad in range(out.shape[0]):
        out[quad] = total


def scan(length, rows, constants, pieces, sums, out):
    span = pieces.shape[1]
    rate = constants[constants.shape[0] - 2][:1]
    decay = jnp.exp(-rate * length)
    whole = jnp.exp(-rate * (length * QUAD))
    mine = lax.axis_index("q")
    carry = jnp.zeros((span, E), F32)
    carries = []
    for row in range(rows):
        for quad in range(sums.shape[0]):
            chosen = carry if quad == 0 else jnp.where(mine == quad, carry, chosen)
            some = sums[quad ^ FIRST_QUAD, row * span : (row + 1) * span, :]
            carry = carry * whole + some.astype(F32)
        carries.append(chosen)
    total = jnp.concatenate(carries, axis=0)
    for step in range(QUAD):
        rounded = total.astype(BF)
        for row in range(rows):
            slot = (row * QUAD + step) ^ FIRST_AFTER
            out[slot] = rounded[row * span : (row + 1) * span]
        total = total * decay + at_step(pieces, step)


def finish(tokens, constants, positions, received, prior, sums, query_weight, out):
    heads = received.shape[2] // E
    groups = received.shape[0]
    ones = jnp.full((E, E), 1.0 / E, BF)

    def add(head, own, weight):
        slots = [(head * QUAD + part) ^ FIRST_AFTER for part in range(QUAD)]
        state = jnp.concatenate([prior[slot] for slot in slots], axis=0)
        query_rows = rows_of(received, tokens, 0, head)
        combined = own + jnp.dot(query_rows, state, preferred_element_type=F32) * weight
        square = jnp.dot(
            (combined * combined).astype(BF), ones, preferred_element_type=F32
        )
        scaling = constants[2 * head + 1][:1]
        normal = (combined * lax.rsqrt(square + 1e-06) * scaling).astype(BF)
        columns = slice(head * E, (head + 1) * E)
        for slot in range(groups):
            to = slot ^ FIRST_GROUP ^ LAST_GROUP
            out[to, :, columns] = normal[slot * tokens : (slot + 1) * tokens]

    @pl.when(lax.axis_index("q") != FIRST_QUAD)
    def _():
        for head in range(heads):
            add(head, sums[head], query_weight[:, head : head + 1])

    @pl.when(lax.axis_index("q") == FIRST_QUAD)
    def _():
        for head in range(heads):
            decay = constants[2 * head][:1]
            add(head, *within(tokens, decay, positions, received, head))


def unpack(received, out, sem):
    width = received.shape[2]
    for slot in range(received.shape[0]):
        columns = out.at[0, :, pl.ds((slot ^ LAST_GROUP) * width, width)]
        pltpu.make_async_copy(received.at[slot], columns, sem).start()
    pltpu.make_async_copy(received, received, sem).wait()


def exchange(value, axis, first):
    order = [[at ^ first for at in range(value.shape[0])]]
    return lax.all_to_all(
        value, axis, split_axis=0, concat_axis=0, tiled=True, axis_index_groups=order
    )


def on_device(query, keys, values, decay_exp, gain, route):
    groups = lax.axis_size("group")
    rows = lax.axis_size("x")
    tokens, width = query.shape[1:]
    all_heads = decay_exp.shape[0]
    heads = all_heads // groups
    length = tokens * groups
    scale = 1.0 / (4.0 * length * rows * QUADS * QUAD)
    span = E // QUAD
    sent, positions = pl.pallas_call(
        functools.partial(pack, tokens, width // groups),
        in_specs=[anywhere()] * 4,
        out_specs=(vmem(), vmem()),
        out_shape=(
            jax.ShapeDtypeStruct((groups, 3 * tokens, width // groups), BF),
            jax.ShapeDtypeStruct((ROW, length), F32),
        ),
        scratch_shapes=[
            pltpu.SMEM(route.shape, jnp.int32),
            pltpu.SemaphoreType.DMA((4,)),
        ],
        compiler_params=params(),
        name="pack",
    )(*[pltpu.with_memory_space_constraint(x, pltpu.HBM) for x in (route, query, keys, values)])
    received = exchange(sent, "group", FIRST_GROUP)
    sliced, constants, sums, query_weight = pl.pallas_call(
        functools.partial(states, tokens, scale),
        in_specs=[vmem()] * 4,
        out_specs=(vmem(),) * 4,
        out_shape=(
            jax.ShapeDtypeStruct((heads * QUAD, span, E), BF),
            jax.ShapeDtypeStruct((2 * heads + 2, ROW, E), F32),
            jax.ShapeDtypeStruct((heads, length, E), F32),
            jax.ShapeDtypeStruct((length, E), F32),
        ),
        compiler_params=params(),
        name="states",
    )(decay_exp.reshape(1, all_heads), gain.reshape(all_heads, E), positions, received)
    sliced = exchange(sliced, ("x", "r"), FIRST_BEFORE)
    quads = pl.pallas_call(
        functools.partial(totals, length),
        in_specs=[vmem(), vmem()],
        out_specs=vmem(),
        out_shape=jax.ShapeDtypeStruct((QUADS, rows * span, E), BF),
        compiler_params=params(),
        name="totals",
    )(constants, sliced)
    quads = exchange(quads, "q", FIRST_QUAD)
    priors = pl.pallas_call(
        functools.partial(scan, length, rows),
        in_specs=[vmem(), vmem(), vmem()],
        out_specs=vmem(),
        out_shape=jax.ShapeDtypeStruct((rows * QUAD, span, E), BF),
        compiler_params=params(),
        name="scan",
    )(constants, sliced, quads)
    priors = exchange(priors, ("x", "r"), FIRST_AFTER)
    mixed = pl.pallas_call(
        functools.partial(finish, tokens),
        in_specs=[vmem()] * 6,
        out_specs=vmem(),
        out_shape=jax.ShapeDtypeStruct((groups, tokens, width // groups), BF),
        compiler_params=params(),
        name="finish",
    )(constants, positions, received, priors, sums, query_weight)
    mixed = exchange(mixed, "group", LAST_GROUP)
    return pl.pallas_call(
        unpack,
        in_specs=[anywhere()],
        out_specs=anywhere(),
        out_shape=jax.ShapeDtypeStruct((1, tokens, width), BF),
        scratch_shapes=[pltpu.SemaphoreType.DMA],
        compiler_params=params(),
        name="unpack",
    )(mixed)


def solution(mesh):
    devices = np.asarray(mesh.devices)
    split = Mesh(
        devices.reshape(devices.shape[0], -1, QUADS, QUAD), ("group", "x", "q", "r")
    )
    ctx = ("x", "q", "r")
    stored = P("group", ctx, None)
    in_specs = (stored, stored, stored, P(), P(), P(None, ctx, None))
    return jax.shard_map(
        on_device, mesh=split, in_specs=in_specs, out_specs=stored, check_vma=False
    )
```

```python
import functools

import jax
import jax.numpy as jnp
import numpy as np
from jax import lax
from jax.experimental import pallas as pl
from jax.experimental.pallas import tpu as pltpu
from jax.sharding import Mesh
from jax.sharding import PartitionSpec as P

BF = jnp.bfloat16
F32 = jnp.float32
QUADS = 4
QUAD = 4
E = 128
ROW = 8
FIRST_GROUP, LAST_GROUP, FIRST_QUAD = 7, 5, 2
FIRST_BEFORE, FIRST_AFTER = 10, 10


LATE_QUADS = (2, 3)


def vmem():
    return pl.BlockSpec(memory_space=pltpu.VMEM)


def params(mebibytes=48):
    return pltpu.CompilerParams(vmem_limit_bytes=mebibytes * 1024 * 1024)


def anywhere():
    return pl.BlockSpec(memory_space=pl.ANY)


def pack(tokens, width, route, query, keys, values, out, positions, route_ref, sems):
    groups = out.shape[0]
    fetch = pltpu.make_async_copy(route, route_ref, sems.at[3])
    fetch.start()
    for at, source in enumerate((query, keys, values)):
        for slot in range(groups):
            pltpu.make_async_copy(
                source.at[0, :, pl.ds((slot ^ FIRST_GROUP) * width, width)],
                out.at[slot, pl.ds(at * tokens, tokens), :],
                sems.at[at],
            ).start()
    lane = lax.broadcasted_iota(jnp.int32, (ROW, E), 1)
    per_slot = tokens // ROW
    fetch.wait()
    for chunk in range(groups * tokens // E):
        places = jnp.zeros((ROW, E), jnp.int32)
        for piece in range(E // ROW):
            slot, own = divmod(chunk * (E // ROW) + piece, per_slot)
            place = route_ref[slot ^ FIRST_GROUP, 0, own]
            places = jnp.where(lane // ROW == piece, place, places)
        positions[:, chunk * E : (chunk + 1) * E] = (places * ROW + lane % ROW).astype(F32)
    for at in range(3):
        landed = out.at[:, pl.ds(at * tokens, tokens), :]
        pltpu.make_async_copy(landed, landed, sems.at[at]).wait()


def is_late():
    quad = lax.axis_index("q")
    return (quad >= LATE_QUADS[0]) & (quad <= LATE_QUADS[-1])


def rows_of(received, tokens, which, head):
    part = received[
        :, which * tokens : (which + 1) * tokens, head * E : (head + 1) * E
    ]
    return part.reshape(received.shape[0] * tokens, E)


def within(tokens, decay, positions, received, head):
    length = received.shape[0] * tokens
    middle = length / 2.0
    row = positions[:1, :]
    chunks = [
        jnp.transpose(jnp.broadcast_to(row[:, at : at + E], (E, E)))
        for at in range(0, length, E)
    ]
    column = jnp.concatenate(chunks, axis=0)
    wide = jnp.concatenate([decay] * (length // E), axis=1)
    key_weight = jnp.exp(wide * (row - middle))
    weight = jnp.exp(-decay * (column - middle))
    scores = lax.dot_general(
        rows_of(received, tokens, 0, head),
        rows_of(received, tokens, 1, head),
        (((1,), (1,)), ((), ())),
        preferred_element_type=F32,
    )
    weights = jnp.where(column[:, :1] >= row, scores * key_weight, 0.0).astype(BF)
    values = rows_of(received, tokens, 2, head)
    sums = jnp.dot(weights, values, preferred_element_type=F32) * weight
    return sums, weight * jnp.exp(-decay * (middle + 1.0))


def states(
    tokens, scale, exponents, gain, positions, received, out, constants, sums, query_weight
):
    heads = received.shape[2] // E
    length = received.shape[0] * tokens
    all_heads = exponents.shape[1]
    first = lax.axis_index("group") * heads
    for at in range(heads + 1):
        head = first + (at if at < heads else lax.axis_index("x"))
        mine = lax.broadcasted_iota(jnp.int32, (1, all_heads), 1) == head
        exponent = jnp.sum(
            jnp.where(mine, exponents[...], 0).astype(F32), axis=1, keepdims=True
        )
        exponent = jnp.broadcast_to(exponent, (ROW, E))
        constants[2 * at] = jnp.exp2(exponent * exponent / 8.0) * scale
        if at < heads:
            constants[2 * at + 1] = jnp.broadcast_to(gain[pl.ds(head, 1), :], (ROW, E))
    found = []
    for head in range(heads):
        wide = jnp.concatenate([constants[2 * head][:1]] * (length // E), axis=1)
        weight = jnp.exp(-wide * (length - 1.0 - positions[:1, :]))
        key_rows = rows_of(received, tokens, 1, head)
        weighted = (jnp.transpose(key_rows).astype(F32) * weight).astype(BF)
        values = rows_of(received, tokens, 2, head)
        found.append(jnp.dot(weighted, values, preferred_element_type=F32).astype(BF))
    span = out.shape[1]
    for slot in range(out.shape[0]):
        head, part = divmod(slot ^ FIRST_BEFORE, QUAD)
        out[slot] = found[head][part * span : (part + 1) * span]

    @pl.when(jnp.logical_not(is_late()))
    def _():
        lane = lax.broadcasted_iota(jnp.int32, (length, E), 1)
        weights = jnp.zeros((length, E), F32)
        for head in range(heads):
            decay = constants[2 * head][:1]
            sums[head], weight = within(tokens, decay, positions, received, head)
            weights = jnp.where(lane == head, weight, weights)
        query_weight[...] = weights


def at_step(pieces, step):
    rows = pieces.shape[0] // QUAD
    slots = [(row * QUAD + step) ^ FIRST_BEFORE for row in range(rows)]
    return jnp.concatenate([pieces[slot] for slot in slots], axis=0).astype(F32)


def totals(length, constants, pieces, out):
    decay = jnp.exp(-constants[constants.shape[0] - 2][:1] * length)
    total = at_step(pieces, 0)
    for step in range(1, QUAD):
        total = total * decay + at_step(pieces, step)
    total = total.astype(BF)
    for quad in range(out.shape[0]):
        out[quad] = total


def scan(length, rows, constants, pieces, sums, out):
    span = pieces.shape[1]
    rate = constants[constants.shape[0] - 2][:1]
    decay = jnp.exp(-rate * length)
    whole = jnp.exp(-rate * (length * QUAD))
    mine = lax.axis_index("q")
    carry = jnp.zeros((span, E), F32)
    carries = []
    for row in range(rows):
        for quad in range(sums.shape[0]):
            chosen = carry if quad == 0 else jnp.where(mine == quad, carry, chosen)
            some = sums[quad ^ FIRST_QUAD, row * span : (row + 1) * span, :]
            carry = carry * whole + some.astype(F32)
        carries.append(chosen)
    total = jnp.concatenate(carries, axis=0)
    for step in range(QUAD):
        rounded = total.astype(BF)
        for row in range(rows):
            slot = (row * QUAD + step) ^ FIRST_AFTER
            out[slot] = rounded[row * span : (row + 1) * span]
        total = total * decay + at_step(pieces, step)


def finish(tokens, constants, positions, received, prior, sums, query_weight, out):
    heads = received.shape[2] // E
    groups = received.shape[0]
    ones = jnp.full((E, E), 1.0 / E, BF)

    def add(head, own, weight):
        slots = [(head * QUAD + part) ^ FIRST_AFTER for part in range(QUAD)]
        state = jnp.concatenate([prior[slot] for slot in slots], axis=0)
        query_rows = rows_of(received, tokens, 0, head)
        combined = own + jnp.dot(query_rows, state, preferred_element_type=F32) * weight
        square = jnp.dot(
            (combined * combined).astype(BF), ones, preferred_element_type=F32
        )
        scaling = constants[2 * head + 1][:1]
        normal = (combined * lax.rsqrt(square + 1e-06) * scaling).astype(BF)
        columns = slice(head * E, (head + 1) * E)
        for slot in range(groups):
            to = slot ^ FIRST_GROUP ^ LAST_GROUP
            out[to, :, columns] = normal[slot * tokens : (slot + 1) * tokens]

    @pl.when(jnp.logical_not(is_late()))
    def _():
        for head in range(heads):
            add(head, sums[head], query_weight[:, head : head + 1])

    @pl.when(is_late())
    def _():
        for head in range(heads):
            decay = constants[2 * head][:1]
            add(head, *within(tokens, decay, positions, received, head))


def unpack(received, out, sem):
    width = received.shape[2]
    for slot in range(received.shape[0]):
        columns = out.at[0, :, pl.ds((slot ^ LAST_GROUP) * width, width)]
        pltpu.make_async_copy(received.at[slot], columns, sem).start()
    pltpu.make_async_copy(received, received, sem).wait()


def exchange(value, axis, first):
    order = [[at ^ first for at in range(value.shape[0])]]
    return lax.all_to_all(
        value, axis, split_axis=0, concat_axis=0, tiled=True, axis_index_groups=order
    )


def on_device(query, keys, values, decay_exp, gain, route):
    groups = lax.axis_size("group")
    rows = lax.axis_size("x")
    tokens, width = query.shape[1:]
    all_heads = decay_exp.shape[0]
    heads = all_heads // groups
    length = tokens * groups
    scale = 1.0 / (4.0 * length * rows * QUADS * QUAD)
    span = E // QUAD
    sent, positions = pl.pallas_call(
        functools.partial(pack, tokens, width // groups),
        in_specs=[anywhere()] * 4,
        out_specs=(vmem(), vmem()),
        out_shape=(
            jax.ShapeDtypeStruct((groups, 3 * tokens, width // groups), BF),
            jax.ShapeDtypeStruct((ROW, length), F32),
        ),
        scratch_shapes=[
            pltpu.SMEM(route.shape, jnp.int32),
            pltpu.SemaphoreType.DMA((4,)),
        ],
        compiler_params=params(),
        name="pack",
    )(*[pltpu.with_memory_space_constraint(x, pltpu.HBM) for x in (route, query, keys, values)])
    received = exchange(sent, "group", FIRST_GROUP)
    sliced, constants, sums, query_weight = pl.pallas_call(
        functools.partial(states, tokens, scale),
        in_specs=[vmem()] * 4,
        out_specs=(vmem(),) * 4,
        out_shape=(
            jax.ShapeDtypeStruct((heads * QUAD, span, E), BF),
            jax.ShapeDtypeStruct((2 * heads + 2, ROW, E), F32),
            jax.ShapeDtypeStruct((heads, length, E), F32),
            jax.ShapeDtypeStruct((length, E), F32),
        ),
        compiler_params=params(),
        name="states",
    )(decay_exp.reshape(1, all_heads), gain.reshape(all_heads, E), positions, received)
    sliced = exchange(sliced, ("x", "r"), FIRST_BEFORE)
    quads = pl.pallas_call(
        functools.partial(totals, length),
        in_specs=[vmem(), vmem()],
        out_specs=vmem(),
        out_shape=jax.ShapeDtypeStruct((QUADS, rows * span, E), BF),
        compiler_params=params(),
        name="totals",
    )(constants, sliced)
    quads = exchange(quads, "q", FIRST_QUAD)
    priors = pl.pallas_call(
        functools.partial(scan, length, rows),
        in_specs=[vmem(), vmem(), vmem()],
        out_specs=vmem(),
        out_shape=jax.ShapeDtypeStruct((rows * QUAD, span, E), BF),
        compiler_params=params(),
        name="scan",
    )(constants, sliced, quads)
    priors = exchange(priors, ("x", "r"), FIRST_AFTER)
    mixed = pl.pallas_call(
        functools.partial(finish, tokens),
        in_specs=[vmem()] * 6,
        out_specs=vmem(),
        out_shape=jax.ShapeDtypeStruct((groups, tokens, width // groups), BF),
        compiler_params=params(),
        name="finish",
    )(constants, positions, received, priors, sums, query_weight)
    mixed = exchange(mixed, "group", LAST_GROUP)
    return pl.pallas_call(
        unpack,
        in_specs=[anywhere()],
        out_specs=anywhere(),
        out_shape=jax.ShapeDtypeStruct((1, tokens, width), BF),
        scratch_shapes=[pltpu.SemaphoreType.DMA],
        compiler_params=params(),
        name="unpack",
    )(mixed)


def solution(mesh):
    devices = np.asarray(mesh.devices)
    split = Mesh(
        devices.reshape(devices.shape[0], -1, QUADS, QUAD), ("group", "x", "q", "r")
    )
    ctx = ("x", "q", "r")
    stored = P("group", ctx, None)
    in_specs = (stored, stored, stored, P(), P(), P(None, ctx, None))
    return jax.shard_map(
        on_device, mesh=split, in_specs=in_specs, out_specs=stored, check_vma=False
    )
```

```python
import functools

import jax
import jax.numpy as jnp
import numpy as np
from jax import lax
from jax.experimental import pallas as pl
from jax.experimental.pallas import tpu as pltpu
from jax.sharding import Mesh
from jax.sharding import PartitionSpec as P

BF = jnp.bfloat16
F32 = jnp.float32
QUADS = 4
QUAD = 4
E = 128
ROW = 8
FIRST_GROUP, LAST_GROUP, FIRST_QUAD = 7, 5, 2
FIRST_BEFORE, FIRST_AFTER = 10, 10


LATE_QUADS = (1, 3)


def vmem():
    return pl.BlockSpec(memory_space=pltpu.VMEM)


def params(mebibytes=48):
    return pltpu.CompilerParams(vmem_limit_bytes=mebibytes * 1024 * 1024)


def anywhere():
    return pl.BlockSpec(memory_space=pl.ANY)


def pack(tokens, width, route, query, keys, values, out, positions, route_ref, sems):
    groups = out.shape[0]
    fetch = pltpu.make_async_copy(route, route_ref, sems.at[3])
    fetch.start()
    for at, source in enumerate((query, keys, values)):
        for slot in range(groups):
            pltpu.make_async_copy(
                source.at[0, :, pl.ds((slot ^ FIRST_GROUP) * width, width)],
                out.at[slot, pl.ds(at * tokens, tokens), :],
                sems.at[at],
            ).start()
    lane = lax.broadcasted_iota(jnp.int32, (ROW, E), 1)
    per_slot = tokens // ROW
    fetch.wait()
    for chunk in range(groups * tokens // E):
        places = jnp.zeros((ROW, E), jnp.int32)
        for piece in range(E // ROW):
            slot, own = divmod(chunk * (E // ROW) + piece, per_slot)
            place = route_ref[slot ^ FIRST_GROUP, 0, own]
            places = jnp.where(lane // ROW == piece, place, places)
        positions[:, chunk * E : (chunk + 1) * E] = (places * ROW + lane % ROW).astype(F32)
    for at in range(3):
        landed = out.at[:, pl.ds(at * tokens, tokens), :]
        pltpu.make_async_copy(landed, landed, sems.at[at]).wait()


def is_late():
    quad = lax.axis_index("q")
    return (quad >= LATE_QUADS[0]) & (quad <= LATE_QUADS[-1])


def rows_of(received, tokens, which, head):
    part = received[
        :, which * tokens : (which + 1) * tokens, head * E : (head + 1) * E
    ]
    return part.reshape(received.shape[0] * tokens, E)


def within(tokens, decay, positions, received, head):
    length = received.shape[0] * tokens
    middle = length / 2.0
    row = positions[:1, :]
    chunks = [
        jnp.transpose(jnp.broadcast_to(row[:, at : at + E], (E, E)))
        for at in range(0, length, E)
    ]
    column = jnp.concatenate(chunks, axis=0)
    wide = jnp.concatenate([decay] * (length // E), axis=1)
    key_weight = jnp.exp(wide * (row - middle))
    weight = jnp.exp(-decay * (column - middle))
    scores = lax.dot_general(
        rows_of(received, tokens, 0, head),
        rows_of(received, tokens, 1, head),
        (((1,), (1,)), ((), ())),
        preferred_element_type=F32,
    )
    weights = jnp.where(column[:, :1] >= row, scores * key_weight, 0.0).astype(BF)
    values = rows_of(received, tokens, 2, head)
    sums = jnp.dot(weights, values, preferred_element_type=F32) * weight
    return sums, weight * jnp.exp(-decay * (middle + 1.0))


def states(
    tokens, scale, exponents, gain, positions, received, out, constants, sums, query_weight
):
    heads = received.shape[2] // E
    length = received.shape[0] * tokens
    all_heads = exponents.shape[1]
    first = lax.axis_index("group") * heads
    for at in range(heads + 1):
        head = first + (at if at < heads else lax.axis_index("x"))
        mine = lax.broadcasted_iota(jnp.int32, (1, all_heads), 1) == head
        exponent = jnp.sum(
            jnp.where(mine, exponents[...], 0).astype(F32), axis=1, keepdims=True
        )
        exponent = jnp.broadcast_to(exponent, (ROW, E))
        constants[2 * at] = jnp.exp2(exponent * exponent / 8.0) * scale
        if at < heads:
            constants[2 * at + 1] = jnp.broadcast_to(gain[pl.ds(head, 1), :], (ROW, E))
    found = []
    for head in range(heads):
        wide = jnp.concatenate([constants[2 * head][:1]] * (length // E), axis=1)
        weight = jnp.exp(-wide * (length - 1.0 - positions[:1, :]))
        key_rows = rows_of(received, tokens, 1, head)
        weighted = (jnp.transpose(key_rows).astype(F32) * weight).astype(BF)
        values = rows_of(received, tokens, 2, head)
        found.append(jnp.dot(weighted, values, preferred_element_type=F32).astype(BF))
    span = out.shape[1]
    for slot in range(out.shape[0]):
        head, part = divmod(slot ^ FIRST_BEFORE, QUAD)
        out[slot] = found[head][part * span : (part + 1) * span]

    @pl.when(jnp.logical_not(is_late()))
    def _():
        lane = lax.broadcasted_iota(jnp.int32, (length, E), 1)
        weights = jnp.zeros((length, E), F32)
        for head in range(heads):
            decay = constants[2 * head][:1]
            sums[head], weight = within(tokens, decay, positions, received, head)
            weights = jnp.where(lane == head, weight, weights)
        query_weight[...] = weights


def at_step(pieces, step):
    rows = pieces.shape[0] // QUAD
    slots = [(row * QUAD + step) ^ FIRST_BEFORE for row in range(rows)]
    return jnp.concatenate([pieces[slot] for slot in slots], axis=0).astype(F32)


def totals(length, constants, pieces, out):
    decay = jnp.exp(-constants[constants.shape[0] - 2][:1] * length)
    total = at_step(pieces, 0)
    for step in range(1, QUAD):
        total = total * decay + at_step(pieces, step)
    total = total.astype(BF)
    for quad in range(out.shape[0]):
        out[quad] = total


def scan(length, rows, constants, pieces, sums, out):
    span = pieces.shape[1]
    rate = constants[constants.shape[0] - 2][:1]
    decay = jnp.exp(-rate * length)
    whole = jnp.exp(-rate * (length * QUAD))
    mine = lax.axis_index("q")
    carry = jnp.zeros((span, E), F32)
    carries = []
    for row in range(rows):
        for quad in range(sums.shape[0]):
            chosen = carry if quad == 0 else jnp.where(mine == quad, carry, chosen)
            some = sums[quad ^ FIRST_QUAD, row * span : (row + 1) * span, :]
            carry = carry * whole + some.astype(F32)
        carries.append(chosen)
    total = jnp.concatenate(carries, axis=0)
    for step in range(QUAD):
        rounded = total.astype(BF)
        for row in range(rows):
            slot = (row * QUAD + step) ^ FIRST_AFTER
            out[slot] = rounded[row * span : (row + 1) * span]
        total = total * decay + at_step(pieces, step)


def finish(tokens, constants, positions, received, prior, sums, query_weight, out):
    heads = received.shape[2] // E
    groups = received.shape[0]
    ones = jnp.full((E, E), 1.0 / E, BF)

    def add(head, own, weight):
        slots = [(head * QUAD + part) ^ FIRST_AFTER for part in range(QUAD)]
        state = jnp.concatenate([prior[slot] for slot in slots], axis=0)
        query_rows = rows_of(received, tokens, 0, head)
        combined = own + jnp.dot(query_rows, state, preferred_element_type=F32) * weight
        square = jnp.dot(
            (combined * combined).astype(BF), ones, preferred_element_type=F32
        )
        scaling = constants[2 * head + 1][:1]
        normal = (combined * lax.rsqrt(square + 1e-06) * scaling).astype(BF)
        columns = slice(head * E, (head + 1) * E)
        for slot in range(groups):
            to = slot ^ FIRST_GROUP ^ LAST_GROUP
            out[to, :, columns] = normal[slot * tokens : (slot + 1) * tokens]

    @pl.when(jnp.logical_not(is_late()))
    def _():
        for head in range(heads):
            add(head, sums[head], query_weight[:, head : head + 1])

    @pl.when(is_late())
    def _():
        for head in range(heads):
            decay = constants[2 * head][:1]
            add(head, *within(tokens, decay, positions, received, head))


def unpack(received, out, sem):
    width = received.shape[2]
    for slot in range(received.shape[0]):
        columns = out.at[0, :, pl.ds((slot ^ LAST_GROUP) * width, width)]
        pltpu.make_async_copy(received.at[slot], columns, sem).start()
    pltpu.make_async_copy(received, received, sem).wait()


def exchange(value, axis, first):
    order = [[at ^ first for at in range(value.shape[0])]]
    return lax.all_to_all(
        value, axis, split_axis=0, concat_axis=0, tiled=True, axis_index_groups=order
    )


def on_device(query, keys, values, decay_exp, gain, route):
    groups = lax.axis_size("group")
    rows = lax.axis_size("x")
    tokens, width = query.shape[1:]
    all_heads = decay_exp.shape[0]
    heads = all_heads // groups
    length = tokens * groups
    scale = 1.0 / (4.0 * length * rows * QUADS * QUAD)
    span = E // QUAD
    sent, positions = pl.pallas_call(
        functools.partial(pack, tokens, width // groups),
        in_specs=[anywhere()] * 4,
        out_specs=(vmem(), vmem()),
        out_shape=(
            jax.ShapeDtypeStruct((groups, 3 * tokens, width // groups), BF),
            jax.ShapeDtypeStruct((ROW, length), F32),
        ),
        scratch_shapes=[
            pltpu.SMEM(route.shape, jnp.int32),
            pltpu.SemaphoreType.DMA((4,)),
        ],
        compiler_params=params(),
        name="pack",
    )(*[pltpu.with_memory_space_constraint(x, pltpu.HBM) for x in (route, query, keys, values)])
    received = exchange(sent, "group", FIRST_GROUP)
    sliced, constants, sums, query_weight = pl.pallas_call(
        functools.partial(states, tokens, scale),
        in_specs=[vmem()] * 4,
        out_specs=(vmem(),) * 4,
        out_shape=(
            jax.ShapeDtypeStruct((heads * QUAD, span, E), BF),
            jax.ShapeDtypeStruct((2 * heads + 2, ROW, E), F32),
            jax.ShapeDtypeStruct((heads, length, E), F32),
            jax.ShapeDtypeStruct((length, E), F32),
        ),
        compiler_params=params(),
        name="states",
    )(decay_exp.reshape(1, all_heads), gain.reshape(all_heads, E), positions, received)
    sliced = exchange(sliced, ("x", "r"), FIRST_BEFORE)
    quads = pl.pallas_call(
        functools.partial(totals, length),
        in_specs=[vmem(), vmem()],
        out_specs=vmem(),
        out_shape=jax.ShapeDtypeStruct((QUADS, rows * span, E), BF),
        compiler_params=params(),
        name="totals",
    )(constants, sliced)
    quads = exchange(quads, "q", FIRST_QUAD)
    priors = pl.pallas_call(
        functools.partial(scan, length, rows),
        in_specs=[vmem(), vmem(), vmem()],
        out_specs=vmem(),
        out_shape=jax.ShapeDtypeStruct((rows * QUAD, span, E), BF),
        compiler_params=params(),
        name="scan",
    )(constants, sliced, quads)
    priors = exchange(priors, ("x", "r"), FIRST_AFTER)
    mixed = pl.pallas_call(
        functools.partial(finish, tokens),
        in_specs=[vmem()] * 6,
        out_specs=vmem(),
        out_shape=jax.ShapeDtypeStruct((groups, tokens, width // groups), BF),
        compiler_params=params(),
        name="finish",
    )(constants, positions, received, priors, sums, query_weight)
    mixed = exchange(mixed, "group", LAST_GROUP)
    return pl.pallas_call(
        unpack,
        in_specs=[anywhere()],
        out_specs=anywhere(),
        out_shape=jax.ShapeDtypeStruct((1, tokens, width), BF),
        scratch_shapes=[pltpu.SemaphoreType.DMA],
        compiler_params=params(),
        name="unpack",
    )(mixed)


def solution(mesh):
    devices = np.asarray(mesh.devices)
    split = Mesh(
        devices.reshape(devices.shape[0], -1, QUADS, QUAD), ("group", "x", "q", "r")
    )
    ctx = ("x", "q", "r")
    stored = P("group", ctx, None)
    in_specs = (stored, stored, stored, P(), P(), P(None, ctx, None))
    return jax.shard_map(
        on_device, mesh=split, in_specs=in_specs, out_specs=stored, check_vma=False
    )
```
